32 devices in a mesh: dp: 16 (over z, y, x), mp: 2 (over core).
Axes of the slice: x: 2, y: 2, z: 4, core: 2. Of those that a mesh axis runs over, the one named last changes fastest.
Arguments:
- tokens: bfloat16 [32768, 512], P(('dp', 'mp')), may hold values from -6 to 6
- cotangent: bfloat16 [32768, 512], P(('dp', 'mp')), may hold values from -6 to 6
- block_kinds: int32 [256], P(('dp', 'mp')), may hold values from 0 to 1, as said below
- qkv_weight: bfloat16 [2, 512, 1536], replicated, may hold values from -0.25 to 0.25
- out_weight: bfloat16 [2, 512, 512], replicated, may hold values from -0.75 to 0.75
- attn_bias: float32 [2, 3, 512], replicated, may hold values from -3 to 3
- norm_gain: float32 [2, 2, 512], replicated, may hold values from 0.5 to 1.5
- norm_bias: float32 [2, 2, 512], replicated, may hold values from -2 to 2
- up_weight: bfloat16 [2, 512, 2048], P(None, None, 'mp'), may hold values from -0.25 to 0.25
- up_bias: float32 [2, 2048], P(None, 'mp'), may hold values from -3 to 3
- down_weight: bfloat16 [2, 2048, 512], P(None, 'mp'), may hold values from -0.125 to 0.125
- down_bias: float32 [2, 512], replicated, may hold values from -2 to 2
Outputs:
- output: bfloat16 [32768, 512], P(('dp', 'mp'))
- input_grad: float32 [32768, 512], P(('dp', 'mp'))
- qkv_weight_grad: float32 [2, 512, 1536], replicated
- out_weight_grad: float32 [2, 512, 512], replicated
- attn_bias_grad: float32 [2, 3, 512], replicated
- norm_gain_grad: float32 [2, 2, 512], replicated
- norm_bias_grad: float32 [2, 2, 512], replicated
- up_weight_grad: float32 [2, 512, 2048], P(None, None, 'mp')
- up_bias_grad: float32 [2, 2048], P(None, 'mp')
- down_weight_grad: float32 [2, 2048, 512], P(None, 'mp')
- down_bias_grad: float32 [2, 512], replicated
The draws below stay inside these ranges and needn't reach their ends.
Inputs may be any that keep to these rules, and one draw needn't show every extreme that they name: `block_kinds`: on each device's 8 groups, groups of kind 1 come before groups of kind 0. The first device's groups are all of kind 1, the second device's all of kind 0.
All inputs are finite; a program needn't handle non-finite values.
Results may differ from the reference program's by a relative error of at most 0.013.
Values may be sent and summed in bfloat16 or wider, within the bound.
No kernel may reach another device: no remote copies, remote signals or barrier semaphores. Data moves between devices by JAX's collectives and lax.ppermute only.
A program may use at most 192 MiB of HBM per device.

```python
import jax
import jax.numpy as jnp
from jax import lax

D = 512
HEADS = 8
HEAD_DIM = 64
FF = 2048
LAYERS = 2
FRAME = 6
SHORT_STEPS = 8
LONG_STEPS = 21
BLK = 128
BLK_DEV = 8
TOKENS = 32768
BLOCKS = 256
N_DP = 16
N_MP = 2


def draw_block_kinds(key, part):
    key = jax.random.fold_in(key, 7)
    device_count = BLOCKS // BLK_DEV
    long_counts = jax.random.randint(key, (device_count,), 0, BLK_DEV + 1)
    long_counts = long_counts.at[0].set(BLK_DEV).at[1].set(0)
    position = jnp.arange(BLK_DEV, dtype=jnp.int32)
    return (position[None, :] < long_counts[:, None]).astype(jnp.int32).reshape(BLOCKS)


def levels(key, shape, shards, low, high):
    loudness = 1.0
    for dim, blocks in shards:
        draws = jax.random.uniform(jax.random.fold_in(jax.random.fold_in(key, 6), dim), (blocks,), jnp.float32, low / len(shards), high / len(shards))
        loudness = loudness * jnp.repeat(jnp.exp(draws), shape[dim] // blocks).reshape((-1,) + (1,) * (len(shape) - 1 - dim))
    return loudness


def noise(stream_key, shape, scale, bound, shards=(), kind=jnp.bfloat16):
    values = jax.random.normal(stream_key, shape, jnp.float32) * scale
    if len(shards) > 0:
        values = levels(stream_key, shape, shards, -0.22, 0.18) * values
    return jnp.clip(values, min=-bound, max=bound).astype(kind)


def setup_inputs(seed: int = 0) -> dict:
    arg_keys = jax.random.split(jax.random.key(seed), 13)
    tokens = noise(arg_keys[0], (TOKENS, D), 1.0, 6.0, ((0, 32),))
    cotangent = noise(arg_keys[1], (TOKENS, D), 1.0, 6.0, ((0, 32),))
    block_kinds = draw_block_kinds(jax.random.fold_in(arg_keys[12], 71), 0)
    qkv_weight = noise(arg_keys[3], (LAYERS, D, 3 * D), D ** -0.5, 0.25)
    out_weight = noise(arg_keys[4], (LAYERS, D, D), (D // 8) ** -0.5, 0.75)
    attn_bias = noise(arg_keys[5], (LAYERS, 3, D), 0.5, 3.0, (), jnp.float32)
    norm_gain = jnp.clip(1.0 + 0.1 * jax.random.normal(arg_keys[6], (LAYERS, 2, D), jnp.float32), 0.5, 1.5)
    norm_bias = noise(arg_keys[7], (LAYERS, 2, D), 0.3, 2.0, (), jnp.float32)
    up_weight = noise(arg_keys[8], (LAYERS, D, FF), D ** -0.5, 0.25, ((2, 2),))
    up_bias = noise(arg_keys[9], (LAYERS, FF), 0.5, 3.0, ((1, 2),), jnp.float32)
    down_weight = noise(arg_keys[10], (LAYERS, FF, D), FF ** -0.5, 0.125, ((1, 2),))
    down_bias = noise(arg_keys[11], (LAYERS, D), 0.3, 2.0, (), jnp.float32)
    return {"tokens": tokens, "cotangent": cotangent, "block_kinds": block_kinds, "qkv_weight": qkv_weight, "out_weight": out_weight, "attn_bias": attn_bias, "norm_gain": norm_gain, "norm_bias": norm_bias, "up_weight": up_weight, "up_bias": up_bias, "down_weight": down_weight, "down_bias": down_bias}


@jax.custom_vjp
def low(v):
    return lax.optimization_barrier(v.astype(jnp.bfloat16)).astype(jnp.float32)

@jax.custom_vjp
def low_back(v):
    return v

def low_keep(v):
    return (low(v), None)

def low_pass(kept, grad):
    return (grad,)

def back_keep(v):
    return (v, None)

def back_low(kept, grad):
    return (low(grad),)
low.defvjp(low_keep, low_pass)
low_back.defvjp(back_keep, back_low)
EPSILON = 1e-05
HIGHEST = lax.Precision.HIGHEST

def round_both(value):
    return low_back(low(value))

def layer_norm(stream, gain_vec, shift_vec):
    centered = stream - lax.optimization_barrier(jnp.mean(stream, axis=-1, keepdims=True))
    inv_std = lax.rsqrt(lax.optimization_barrier(jnp.mean(centered * centered, axis=-1, keepdims=True)) + EPSILON)
    return centered * inv_std * gain_vec + shift_vec

def layout(block_kinds):
    block_count = block_kinds.shape[0]
    position = jnp.arange(BLK, dtype=jnp.int32)[None, :]
    short_len = SHORT_STEPS * FRAME
    is_long = block_kinds[:, None] == 1
    seq_ids = jnp.where(is_long, 0, position // short_len) + 2 * jnp.arange(block_count, dtype=jnp.int32)[:, None]
    valid_slot = jnp.where(is_long, position < LONG_STEPS * FRAME, position < 2 * short_len)
    step_ids = jnp.where(is_long, position // FRAME, position % short_len // FRAME)
    return (seq_ids.reshape(-1), step_ids.reshape(-1), valid_slot.reshape(-1))

def tile_mask(seq_ids, step_ids, valid_slot):
    slot_count = seq_ids.shape[-1]
    same_seq = seq_ids[..., :, None] == seq_ids[..., None, :]
    earlier = step_ids[..., None, :] <= step_ids[..., :, None]
    both_valid = valid_slot[..., :, None] & valid_slot[..., None, :]
    return same_seq & earlier & both_valid | jnp.eye(slot_count, dtype=bool)

def attend_tile(operands):
    query, key_rows, values, seq_ids, step_ids, valid_slot = operands
    allowed = tile_mask(seq_ids, step_ids, valid_slot)
    scores = jnp.einsum('gqhd,gkhd->ghqk', query, key_rows, precision=HIGHEST) * HEAD_DIM ** (-0.5)
    scores = low_back(scores)
    scores = jnp.where(allowed[:, None], scores, -1e+30)
    row_max = lax.optimization_barrier(jnp.max(scores, axis=-1, keepdims=True))
    exp_scores = jnp.exp(scores - row_max)
    attn_probs = low(exp_scores / lax.optimization_barrier(jnp.sum(exp_scores, axis=-1, keepdims=True)))
    return jnp.einsum('ghqk,gkhd->gqhd', attn_probs, values, precision=HIGHEST)

def forward(params, stream, kinds_now):
    qkv_weight, out_weight, attn_bias, norm_gain, norm_bias, up_weight, up_bias, down_weight, down_bias = params
    seq_ids, step_ids, valid_slot = layout(kinds_now)
    row_count = stream.shape[0]
    map_count = row_count // (BLK_DEV * BLK)

    def to_tiles(array_in):
        return array_in.reshape((map_count, BLK_DEV, BLK) + array_in.shape[1:])
    attend = jax.checkpoint(attend_tile)
    for layer_no in range(LAYERS):
        hidden = low(layer_norm(stream, norm_gain[layer_no, 0], norm_bias[layer_no, 0]))
        qkv_bias = jnp.concatenate([attn_bias[layer_no, 0], jnp.zeros((D,), jnp.float32), attn_bias[layer_no, 1]])
        qkv = round_both(jnp.dot(hidden, qkv_weight[layer_no], precision=HIGHEST) + qkv_bias)
        head_view = qkv.reshape(row_count, 3, HEADS, HEAD_DIM)
        mixed_out = lax.map(attend, (to_tiles(head_view[:, 0]), to_tiles(head_view[:, 1]), to_tiles(head_view[:, 2]), to_tiles(seq_ids), to_tiles(step_ids), to_tiles(valid_slot)))
        mixed_out = round_both(mixed_out.reshape(row_count, D))
        stream = stream + low_back(jnp.dot(mixed_out, out_weight[layer_no], precision=HIGHEST) + attn_bias[layer_no, 2])
        inner_norm = low(layer_norm(stream, norm_gain[layer_no, 1], norm_bias[layer_no, 1]))
        pre_act = low_back(jnp.dot(inner_norm, up_weight[layer_no], precision=HIGHEST) + up_bias[layer_no])
        activated = low(jax.nn.gelu(pre_act, approximate=False))
        stream = stream + low_back(jnp.dot(activated, down_weight[layer_no], precision=HIGHEST) + down_bias[layer_no])
    return stream

def reference(tokens, cotangent, block_kinds, qkv_weight, out_weight, attn_bias, norm_gain, norm_bias, up_weight, up_bias, down_weight, down_bias):
    params = tuple((array_in.astype(jnp.float32) for array_in in (qkv_weight, out_weight, attn_bias, norm_gain, norm_bias, up_weight, up_bias, down_weight, down_bias)))
    group_rows = N_MP * BLK_DEV * BLK
    stream = tokens.astype(jnp.float32).reshape(N_DP, group_rows, D)
    grads_in = cotangent.astype(jnp.float32).reshape(N_DP, group_rows, D)
    kinds_grouped = block_kinds.reshape(N_DP, N_MP * BLK_DEV)

    def one_group(totals, operands):
        rows_in, rows_grad, kinds_now = operands

        def group_forward(param_set, stream_in):
            return forward(param_set, stream_in, kinds_now)
        result, pullback = jax.vjp(group_forward, params, rows_in)
        param_grads, input_grad = pullback(rows_grad)
        totals = jax.tree.map(jnp.add, totals, param_grads)
        return (totals, (result, input_grad))
    zero_grads = jax.tree.map(jnp.zeros_like, params)
    totals, (outputs, input_grads) = lax.scan(one_group, zero_grads, (stream, grads_in, kinds_grouped))
    return (outputs.reshape(TOKENS, D).astype(jnp.bfloat16), input_grads.reshape(TOKENS, D), totals[0], totals[1], totals[2], totals[3], totals[4], totals[5], totals[6], totals[7], totals[8])
```

```python
import jax
import jax.numpy as jnp
import numpy as np
from jax import lax
from jax.experimental import pallas as pl
from jax.experimental.pallas import tpu as pltpu
from jax.sharding import PartitionSpec as P

HEADS = 8
HEAD_DIM = 64
LAYERS = 2
FRAME = 6
SHORT_STEPS = 8
LONG_STEPS = 21
BLK = 128
WIDTH = 512
EPSILON = 1e-05
SCALE = HEAD_DIM ** (-0.5)

ROWS = 256
GROUPS = ROWS // BLK
PAIRS = HEADS // 2
PARTS = 16
COLS = 512

F32 = jnp.float32
BF16 = jnp.bfloat16
MIB = 1024 * 1024


def mask_bias():
    position = np.arange(BLK)

    def bias(seq_ids, step_ids, valid):
        allowed = (seq_ids[:, None] == seq_ids[None, :]) & (step_ids[None, :] <= step_ids[:, None])
        allowed &= valid[:, None] & valid[None, :]
        return np.where(allowed | np.eye(BLK, dtype=bool), 0.0, -1e30).astype(np.float32)

    short_len = SHORT_STEPS * FRAME
    short = bias(position // short_len, position % short_len // FRAME, position < 2 * short_len)
    long = bias(0 * position, position // FRAME, position < LONG_STEPS * FRAME)
    return np.stack([short, long])


def dot(a, b):
    return jnp.dot(a, b, preferred_element_type=F32)


def dot_nt(a, b):
    return lax.dot_general(a, b, (((1,), (1,)), ((), ())), preferred_element_type=F32)


def dot_tn(a, b):
    return lax.dot_general(a, b, (((0,), (0,)), ((), ())), preferred_element_type=F32)


def normalize(value):
    centered = value - jnp.mean(value, axis=-1, keepdims=True)
    inv_std = lax.rsqrt(jnp.mean(centered * centered, axis=-1, keepdims=True) + EPSILON)
    return centered * inv_std, inv_std


def norm_backward(grad, gain, normal, inv_std):
    scaled = grad * gain
    first = jnp.mean(scaled, axis=-1, keepdims=True)
    second = jnp.mean(scaled * normal, axis=-1, keepdims=True)
    return inv_std * (scaled - first - normal * second)


def column_sum(value):
    return jnp.sum(value, axis=0, keepdims=True)


def gelu_parts(pre):
    phi = 0.5 + 0.5 * lax.erf(pre * 0.7071067811865476)
    density = jnp.exp(pre * pre * -0.5) * 0.3989422804014327
    return phi, pre * density


def lane_halves(pair):
    lane = lax.broadcasted_iota(jnp.int32, pair.shape, 1)
    zero = jnp.zeros_like(pair)
    return jnp.concatenate(
        [jnp.where(lane < HEAD_DIM, pair, zero), jnp.where(lane < HEAD_DIM, zero, pair)], axis=0
    )


def attention_forward(stream, layer, step, kinds, mask, qkv_w, out_w, ab, ng, nb, qkv, probs, mixed):
    normal, _ = normalize(stream)
    hidden = (normal * ng[layer, 0:1, :] + nb[layer, 0:1, :]).astype(BF16)
    qkv[:, :WIDTH] = (
        (dot(hidden, qkv_w[:, :WIDTH]) + ab[layer, 0:1, :]) * SCALE
    ).astype(BF16)
    qkv[:, WIDTH : 2 * WIDTH] = dot(hidden, qkv_w[:, WIDTH : 2 * WIDTH]).astype(BF16)
    qkv[:, 2 * WIDTH :] = (dot(hidden, qkv_w[:, 2 * WIDTH :]) + ab[layer, 1:2, :]).astype(BF16)
    for group in range(GROUPS):
        rows = slice(group * BLK, (group + 1) * BLK)
        bias = mask[kinds[step * GROUPS + group]]
        for pair in range(PAIRS):
            lanes = slice(pair * BLK, (pair + 1) * BLK)
            query = qkv[rows, lanes]
            keys = lane_halves(qkv[rows, WIDTH + pair * BLK : WIDTH + (pair + 1) * BLK])
            values = lane_halves(qkv[rows, 2 * WIDTH + pair * BLK : 2 * WIDTH + (pair + 1) * BLK])
            scores = dot_nt(query, keys)
            both = []
            for head in range(2):
                part = scores[:, head * BLK : (head + 1) * BLK] + bias
                weights = jnp.exp(part - jnp.max(part, axis=-1, keepdims=True))
                total = jnp.sum(weights, axis=-1, keepdims=True)
                both.append((weights * (1.0 / total)).astype(BF16))
            both = jnp.concatenate(both, axis=1)
            probs[rows, pair * 2 * BLK : (pair + 1) * 2 * BLK] = both
            mixed[rows, lanes] = dot(both, values).astype(BF16)
    return stream + (dot(mixed[...], out_w[...]) + ab[layer, 2:3, :])


def first_kernel(kinds, mask, tokens, qkv_w, out_w, ab, ng, nb, qkv, probs, mixed, middle):
    stream = tokens[...].astype(F32)
    step = pl.program_id(0)
    middle[...] = attention_forward(
        stream, 0, step, kinds, mask, qkv_w, out_w, ab, ng, nb, qkv, probs, mixed
    )


def hidden_blocks(up_own, up_other, down_own, down_other, ub_own, ub_other, layer):
    blocks = []
    for up, down, ub in ((up_own, down_own, ub_own), (up_other, down_other, ub_other)):
        for start in range(0, up.shape[1], COLS):
            cols = slice(start, start + COLS)
            blocks.append((up, down, ub, cols))
    return blocks


def second_kernel(
    kinds, mask, middle, up_own, up_other, down_own, down_other, ub_own, ub_other, db,
    qkv_w, out_w, ab, ng, nb, act, slope, stream_out, qkv, probs, mixed, middle_out,
):
    step = pl.program_id(0)
    value = middle[...]
    normal, _ = normalize(value)
    inner = (normal * ng[0, 1:2, :] + nb[0, 1:2, :]).astype(BF16)
    total = value + db[0:1, :]
    for no, (up, down, ub, cols) in enumerate(
        hidden_blocks(up_own, up_other, down_own, down_other, ub_own, ub_other, 0)
    ):
        pre = dot(inner, up[:, cols]) + ub[0:1, cols]
        phi, tail = gelu_parts(pre)
        active = (pre * phi).astype(BF16)
        act[:, no * COLS : (no + 1) * COLS] = active
        slope[:, no * COLS : (no + 1) * COLS] = (phi + tail).astype(BF16)
        total += dot(active, down[cols, :])
    stream_out[...] = total
    middle_out[...] = attention_forward(
        total, 1, step, kinds, mask, qkv_w, out_w, ab, ng, nb, qkv, probs, mixed
    )


def place_a(rel):
    return (rel & 1) * 8 + ((rel >> 1) & 1) * 4 + (rel >> 2)


def place_b(rel):
    return ((rel >> 1) & 1) * 8 + (rel & 1) * 4 + (rel >> 2)


def piece_a(place):
    return ((place >> 3) & 1) + ((place >> 2) & 1) * 2 + (place & 3) * 4


def piece_b(place):
    return ((place >> 3) & 1) * 2 + ((place >> 2) & 1) + (place & 3) * 4


def feed_forward_sums(
    me, gm, act, gpre, inner, mixed, ga, keep_a, keep_b, send
):
    dp = me[0]
    core = me[1]
    half = act.shape[1] // 2
    rows_a = half // PARTS
    rows_up = WIDTH // PARTS
    rows_out = WIDTH // 2 // PARTS
    for start in range(0, 2 * half, 256):
        tile = dot_tn(act[:, start : start + 256], gm[...]).astype(BF16)
        for j in range(256 // rows_a):
            place = place_a(((start % half) // rows_a + j) ^ dp)
            out = send if start >= half else keep_a
            out[place, 0:rows_a, :] = tile[j * rows_a : (j + 1) * rows_a]
    width_a = rows_a + rows_out
    for top in range(0, WIDTH, 256):
        for start in range(0, 2 * half, COLS):
            tile = dot_tn(inner[:, top : top + 256], gpre[:, start : start + COLS]).astype(BF16)
            lower = (start % half) // COLS * rows_up
            for j in range(256 // rows_up):
                rel = (top // rows_up + j) ^ dp
                piece = tile[j * rows_up : (j + 1) * rows_up]
                if start >= half:
                    send[place_b(rel), width_a + lower : width_a + lower + rows_up, :] = piece
                else:
                    keep_b[place_b(rel), lower : lower + rows_up, :] = piece
    for flip in range(2):
        start = pl.multiple_of((core ^ flip) * 256, 256)
        tile = dot_tn(mixed[:, pl.ds(start, 256)], ga[...]).astype(BF16)
        out = send if flip else keep_a
        for j in range(PARTS):
            out[place_a(j ^ dp), rows_a:width_a, :] = tile[j * rows_out : (j + 1) * rows_out]


def third_kernel(
    me, middle, cot, mixed, up_own, up_other, down_own, down_other, ub_own, ub_other, db, ng, nb,
    output, gmid, keep_a, keep_b, send, small,
    act_s, gpre_s, inner_s, gm_s, mixed_s, ga_s,
):
    step = pl.program_id(0)
    rows = pl.ds(pl.multiple_of(step * ROWS, ROWS), ROWS)

    @pl.when(step == 0)
    def _():
        small[...] = jnp.zeros_like(small)

    value = middle[...]
    normal, inv_std = normalize(value)
    inner = (normal * ng[1, 1:2, :] + nb[1, 1:2, :]).astype(BF16)
    inner_s[rows, :] = inner
    gm = cot[...]
    gm_s[rows, :] = gm
    total = value + db[1:2, :]
    ginner = jnp.zeros((ROWS, WIDTH), F32)
    for no, (up, down, ub, cols) in enumerate(
        hidden_blocks(up_own, up_other, down_own, down_other, ub_own, ub_other, 1)
    ):
        pre = dot(inner, up[:, cols]) + ub[1:2, cols]
        phi, tail = gelu_parts(pre)
        active = (pre * phi).astype(BF16)
        act_s[rows, no * COLS : (no + 1) * COLS] = active
        total += dot(active, down[cols, :])
        gpre = (dot_nt(gm, down[cols, :]) * (phi + tail)).astype(BF16)
        gpre_s[rows, no * COLS : (no + 1) * COLS] = gpre
        small[4 + no : 5 + no, :] += column_sum(gpre.astype(F32))
        ginner += dot_nt(gpre, up[:, cols])
    output[...] = total.astype(BF16)
    grad = gm.astype(F32)
    finish_middle(grad, gm, ginner, normal, inv_std, ng[1, 1:2, :], mixed, gmid, small, mixed_s, ga_s, rows)

    @pl.when(step == pl.num_programs(0) - 1)
    def _():
        feed_forward_sums(
            me, gm_s, act_s, gpre_s, inner_s, mixed_s, ga_s, keep_a, keep_b, send
        )


def finish_middle(grad, gm, ginner, normal, inv_std, gain, mixed, gmid, small, mixed_s, ga_s, rows):
    small[0:1, :] += column_sum(gm.astype(F32))
    small[1:2, :] += column_sum(ginner * normal)
    small[2:3, :] += column_sum(ginner)
    result = grad + norm_backward(ginner, gain, normal, inv_std)
    gmid[...] = result
    ga = result.astype(BF16)
    ga_s[rows, :] = ga
    small[3:4, :] += column_sum(ga.astype(F32))
    mixed_s[rows, :] = mixed[...]


def fifth_kernel(
    me, grad_in, act, slope, middle, mixed, up_own, up_other, down_own, down_other, ng, nb,
    gmid, keep_a, keep_b, send, small,
    act_s, gpre_s, inner_s, gm_s, mixed_s, ga_s,
):
    step = pl.program_id(0)
    rows = pl.ds(pl.multiple_of(step * ROWS, ROWS), ROWS)

    @pl.when(step == 0)
    def _():
        small[...] = jnp.zeros_like(small)

    normal, inv_std = normalize(middle[...])
    inner_s[rows, :] = (normal * ng[0, 1:2, :] + nb[0, 1:2, :]).astype(BF16)
    grad = grad_in[...]
    gm = grad.astype(BF16)
    gm_s[rows, :] = gm
    act_s[rows, :] = act[...]
    ginner = jnp.zeros((ROWS, WIDTH), F32)
    for no, (up, down, _, cols) in enumerate(
        hidden_blocks(up_own, up_other, down_own, down_other, None, None, 0)
    ):
        where = slice(no * COLS, (no + 1) * COLS)
        gpre = (dot_nt(gm, down[cols, :]) * slope[:, where].astype(F32)).astype(BF16)
        gpre_s[rows, where] = gpre
        small[4 + no : 5 + no, :] += column_sum(gpre.astype(F32))
        ginner += dot_nt(gpre, up[:, cols])
    finish_middle(grad, gm, ginner, normal, inv_std, ng[0, 1:2, :], mixed, gmid, small, mixed_s, ga_s, rows)

    @pl.when(step == pl.num_programs(0) - 1)
    def _():
        feed_forward_sums(
            me, gm_s, act_s, gpre_s, inner_s, mixed_s, ga_s, keep_a, keep_b, send
        )


def attention_backward(layer):
    def kernel(
        me, gmid, mixed, qkv, probs, stream, qkv_w, out_w, ng, nb,
        grad_out, keep_a, keep_b, send, small,
        hidden_s, gqkv_s,
    ):
        step = pl.program_id(0)
        start = pl.multiple_of(step * ROWS, ROWS)

        @pl.when(step == 0)
        def _():
            small[...] = jnp.zeros_like(small)

        gmiddle = gmid[...]
        gmixed = dot_nt(gmiddle.astype(BF16), out_w[...]).astype(BF16)
        product = (gmixed.astype(F32) * mixed[...].astype(F32)).astype(BF16)
        row = lax.broadcasted_iota(jnp.int32, (2 * BLK, BLK), 0)
        lane = lax.broadcasted_iota(jnp.int32, (2 * BLK, BLK), 1)
        minus = jnp.where((row < BLK) == (lane < HEAD_DIM), -1.0, 0.0).astype(BF16)
        for group in range(GROUPS):
            rows = slice(group * BLK, (group + 1) * BLK)
            out_rows = pl.ds(start + group * BLK, BLK)
            for pair in range(PAIRS):
                lanes = slice(pair * BLK, (pair + 1) * BLK)
                k_lanes = slice(WIDTH + pair * BLK, WIDTH + (pair + 1) * BLK)
                v_lanes = slice(2 * WIDTH + pair * BLK, 2 * WIDTH + (pair + 1) * BLK)
                gmix = gmixed[rows, lanes]
                left = jnp.concatenate([gmix, product[rows, lanes]], axis=1)
                right = jnp.concatenate([lane_halves(qkv[rows, v_lanes]), minus], axis=1)
                both = probs[rows, pair * 2 * BLK : (pair + 1) * 2 * BLK]
                gscore = (both.astype(F32) * dot_nt(left, right)).astype(BF16)
                gquery = dot(gscore, lane_halves(qkv[rows, k_lanes])) * SCALE
                tall = jnp.concatenate([gscore[:, :BLK], gscore[:, BLK:]], axis=0)
                gkey = dot_tn(tall, lane_halves(qkv[rows, lanes]))
                tall = jnp.concatenate([both[:, :BLK], both[:, BLK:]], axis=0)
                gvalue = dot_tn(tall, lane_halves(gmix))
                gqkv_s[out_rows, lanes] = gquery.astype(BF16)
                gqkv_s[out_rows, k_lanes] = gkey.astype(BF16)
                gqkv_s[out_rows, v_lanes] = gvalue.astype(BF16)
        all_rows = pl.ds(start, ROWS)
        gqkv = gqkv_s[all_rows, :]
        small[0:1, :] += column_sum(gqkv[:, :WIDTH].astype(F32))
        small[1:2, :] += column_sum(gqkv[:, 2 * WIDTH :].astype(F32))
        ghidden = dot_nt(gqkv, qkv_w[...])
        normal, inv_std = normalize(stream[...].astype(F32))
        hidden_s[all_rows, :] = (normal * ng[layer, 0:1, :] + nb[layer, 0:1, :]).astype(BF16)
        small[2:3, :] += column_sum(ghidden * normal)
        small[3:4, :] += column_sum(ghidden)
        grad_out[...] = gmiddle + norm_backward(ghidden, ng[layer, 0:1, :], normal, inv_std)

        @pl.when(step == pl.num_programs(0) - 1)
        def _():
            dp = me[0]
            core = me[1]
            part = WIDTH // 2 // PARTS
            for flip in range(2):
                top = pl.multiple_of((core ^ flip) * 256, 256)
                for block in range(3):
                    tile = dot_tn(
                        hidden_s[:, pl.ds(top, 256)],
                        gqkv_s[:, block * WIDTH : (block + 1) * WIDTH],
                    ).astype(BF16)
                    for j in range(PARTS):
                        piece = tile[j * part : (j + 1) * part]
                        if flip:
                            place = place_b(j ^ dp) if block == 2 else place_a(j ^ dp)
                            send[place, block * part : (block + 1) * part, :] = piece
                        elif block == 2:
                            keep_b[place_b(j ^ dp), :, :] = piece
                        else:
                            keep_a[place_a(j ^ dp), block * part : (block + 1) * part, :] = piece

    return kernel


def tiled(width):
    return pl.BlockSpec((ROWS, width), lambda i, *_: (i, 0))


def fixed(*shape):
    return pl.BlockSpec(shape, lambda i, *_: (0,) * len(shape), pipeline_mode=pl.Buffered(1))


def held(*shape):
    return pl.BlockSpec(shape, lambda i, *_: (0,) * len(shape))


def of_layer(layer, *shape):
    return pl.BlockSpec(
        (None,) + shape, lambda i, *_: (layer,) + (0,) * len(shape), pipeline_mode=pl.Buffered(1)
    )


def call(kernel, name, scalar, steps, ins, outs, scratch=(), vmem=56 * MIB, flops=0, **kwargs):
    return pl.pallas_call(
        kernel,
        name=name,
        grid_spec=pltpu.PrefetchScalarGridSpec(
            num_scalar_prefetch=1,
            grid=(steps,),
            in_specs=[spec for _, spec in ins],
            out_specs=[spec for _, _, spec in outs],
            scratch_shapes=list(scratch),
        ),
        out_shape=[jax.ShapeDtypeStruct(shape, dtype) for shape, dtype, _ in outs],
        compiler_params=pltpu.CompilerParams(
            dimension_semantics=("arbitrary",), vmem_limit_bytes=vmem
        ),
        cost_estimate=pl.CostEstimate(
            flops=flops, bytes_accessed=8 * MIB, transcendentals=0
        ),
        **kwargs,
    )(scalar, *[array for array, _ in ins])


def swap_core(value):
    return lax.ppermute(value, "mp", [(0, 1), (1, 0)])


def swap(value, bit):
    count = lax.axis_size("dp")
    return lax.ppermute(value, "dp", [(i, i ^ bit) for i in range(count)])


def add(*values):
    total = values[0].astype(F32)
    for value in values[1:]:
        total = total + value.astype(F32)
    return total.astype(BF16)


def reduce_pieces(keep_a, keep_b, send):
    rows_a = keep_a.shape[1]
    got = swap_core(send)
    a = add(keep_a, got[:, :rows_a])
    b = add(keep_b, got[:, rows_a:])
    a = add(a[:8], swap(a[8:], 1))
    b = add(b[:8], swap(b[8:], 2))
    a = add(a[:4], swap(a[4:], 2))
    b = add(b[:4], swap(b[4:], 1))
    z = jnp.concatenate([a, b], axis=1)
    own = add(z[0], swap(z[1], 4), swap(z[2], 8), swap(z[3], 12))
    bit = PARTS
    while bit < lax.axis_size("dp"):
        own = add(own, swap(own, bit))
        bit *= 2
    z = jnp.stack([own, swap(own, 4), swap(own, 8), swap(own, 12)])
    a = z[:, :rows_a]
    b = z[:, rows_a:]
    a = jnp.concatenate([a, swap(a, 2)], axis=0)
    b = jnp.concatenate([b, swap(b, 1)], axis=0)
    return (a, swap(a, 1)), (b, swap(b, 2))


def sum_small(own, send):
    total = own + swap_core(send)
    bit = 1
    while bit < lax.axis_size("dp"):
        total = total + swap(total, bit)
        bit *= 2
    return total


def feed_forward_result(layer, half):
    rows_a = half // PARTS
    rows_up = WIDTH // PARTS

    def kernel(me, a0, a1, b0, b1, *refs):
        up, down = refs[-2:]
        dp = me[0]
        for place in range(PARTS):
            a = (a0 if place < 8 else a1)[place % 8]
            top = pl.multiple_of((piece_a(place) ^ dp) * rows_a, rows_a)
            down[pl.ds(top, rows_a), :] = a[:rows_a].astype(F32)
            b = (b0 if place < 8 else b1)[place % 8]
            top = pl.multiple_of((piece_b(place) ^ dp) * rows_up, rows_up)
            for block in range(half // COLS):
                up[pl.ds(top, rows_up), block * COLS : (block + 1) * COLS] = b[
                    block * rows_up : (block + 1) * rows_up
                ].astype(F32)

    return kernel


def shared_result(layer):
    part = WIDTH // 2 // PARTS

    def kernel(me, mine, other, *refs):
        qkv, out = refs[-2:]
        dp = me[0]
        core = me[1]
        for flip, source in enumerate((mine, other)):
            for place in range(PARTS):
                top = (core ^ flip) * (WIDTH // 2) + (piece_a(place) ^ dp) * part
                rows = pl.ds(pl.multiple_of(top, part), part)
                value = source[place]
                for block in range(3):
                    qkv[rows, block * WIDTH : (block + 1) * WIDTH] = value[
                        block * part : (block + 1) * part
                    ].astype(F32)
                out[rows, :] = value[3 * part :].astype(F32)

    return kernel


def call_result(kernel, name, me, layer, arrays, shapes, earlier):
    def whole(array):
        return (array, held(*array.shape))

    outs = [
        (
            (LAYERS,) + shape,
            F32,
            pl.BlockSpec((None,) + shape, lambda i, *_: (layer, 0, 0)),
        )
        for shape in shapes
    ]
    ins = [whole(array) for array in arrays]
    aliases = {}
    if earlier is not None:
        for no, array in enumerate(earlier):
            aliases[1 + len(ins)] = no
            ins.append((array, pl.BlockSpec(memory_space=pl.ANY)))
    return call(kernel, name, me, 1, ins, outs, input_output_aliases=aliases)


def body(
    tokens, cotangent, block_kinds, qkv_weight, out_weight, attn_bias, norm_gain, norm_bias,
    up_weight, up_bias, down_weight, down_bias,
):
    count = tokens.shape[0]
    steps = count // ROWS
    half = up_weight.shape[2]
    full = 2 * half
    mask = (jnp.asarray(mask_bias()), fixed(2, BLK, BLK))
    me = jnp.stack([lax.axis_index("dp") & (PARTS - 1), lax.axis_index("mp")]).astype(jnp.int32)

    up_other = swap_core(up_weight)
    down_other = swap_core(down_weight)
    ub_other = swap_core(up_bias)

    ab = (attn_bias, fixed(*attn_bias.shape))
    ng = (norm_gain, fixed(*norm_gain.shape))
    nb = (norm_bias, fixed(*norm_bias.shape))
    db = (down_bias, fixed(*down_bias.shape))
    ubs = [(up_bias, fixed(*up_bias.shape)), (ub_other, fixed(*up_bias.shape))]

    def attention_weights(layer):
        return [
            (qkv_weight, of_layer(layer, WIDTH, 3 * WIDTH)),
            (out_weight, of_layer(layer, WIDTH, WIDTH)),
        ]

    def hidden_weights(layer):
        return [
            (up_weight, of_layer(layer, WIDTH, half)),
            (up_other, of_layer(layer, WIDTH, half)),
            (down_weight, of_layer(layer, half, WIDTH)),
            (down_other, of_layer(layer, half, WIDTH)),
        ]

    def rows_of(width, dtype):
        return ((count, width), dtype, tiled(width))

    def blocks(array):
        return (array, tiled(array.shape[1]))

    attention_outs = [
        rows_of(3 * WIDTH, BF16),
        rows_of(HEADS * BLK, BF16),
        rows_of(WIDTH, BF16),
        rows_of(WIDTH, F32),
    ]

    qkv0, probs0, mixed0, middle0 = call(
        first_kernel, "attention_forward", block_kinds, steps,
        [mask, blocks(tokens)] + attention_weights(0) + [ab, ng, nb],
        attention_outs,
    )
    act0, slope0, stream1, qkv1, probs1, mixed1, middle1 = call(
        second_kernel, "middle_forward", block_kinds, steps,
        [mask, blocks(middle0)] + hidden_weights(0) + ubs + [db] + attention_weights(1) + [ab, ng, nb],
        [rows_of(full, BF16), rows_of(full, BF16), rows_of(WIDTH, F32)] + attention_outs,
    )

    small_out = ((8, WIDTH), F32, held(8, WIDTH))
    rows_a = half // PARTS + WIDTH // 2 // PARTS
    rows_b = half // PARTS

    def piece_outs(rows_a, rows_b):
        return [
            ((PARTS, rows, WIDTH), BF16, pl.BlockSpec((PARTS, rows, WIDTH), lambda i, *_: (0, 0, 0)))
            for rows in (rows_a, rows_b, rows_a + rows_b)
        ]

    hidden_scratch = [
        pltpu.VMEM((count, full), BF16),
        pltpu.VMEM((count, full), BF16),
    ] + [pltpu.VMEM((count, WIDTH), BF16)] * 4

    output, gmid1, *pieces1, small1 = call(
        third_kernel, "hidden_turn", me, steps,
        [blocks(middle1), blocks(cotangent), blocks(mixed1)] + hidden_weights(1) + ubs + [db, ng, nb],
        [rows_of(WIDTH, BF16), rows_of(WIDTH, F32)] + piece_outs(rows_a, rows_b) + [small_out],
        hidden_scratch,
    )

    part = WIDTH // 2 // PARTS

    def attention_back(layer, gmid, mixed, qkv, probs, stream):
        return call(
            attention_backward(layer), "attention_backward", me, steps,
            [blocks(gmid), blocks(mixed), blocks(qkv), blocks(probs), blocks(stream)]
            + attention_weights(layer) + [ng, nb],
            [rows_of(WIDTH, F32)] + piece_outs(2 * part, part) + [small_out],
            [pltpu.VMEM((count, WIDTH), BF16), pltpu.VMEM((count, 3 * WIDTH), BF16)],
        )

    grad1, *attn_pieces1, attn_small1 = attention_back(1, gmid1, mixed1, qkv1, probs1, stream1)
    gmid0, *pieces0, small0 = call(
        fifth_kernel, "hidden_backward", me, steps,
        [blocks(grad1), blocks(act0), blocks(slope0), blocks(middle0), blocks(mixed0)]
        + hidden_weights(0) + [ng, nb],
        [rows_of(WIDTH, F32)] + piece_outs(rows_a, rows_b) + [small_out],
        hidden_scratch,
    )
    grad0, *attn_pieces0, attn_small0 = attention_back(0, gmid0, mixed0, qkv0, probs0, tokens)

    down_up1 = reduce_pieces(*pieces1)
    shared1 = reduce_pieces(*attn_pieces1)
    down_up0 = reduce_pieces(*pieces0)
    shared0 = reduce_pieces(*attn_pieces0)

    hidden_result = None
    shared_out = None
    for layer, ((a, b), (c, d)) in ((1, (down_up1, shared1)), (0, (down_up0, shared0))):
        hidden_result = call_result(
            feed_forward_result(layer, half), "hidden_result", me, layer, list(a) + list(b),
            [(WIDTH, half), (half, WIDTH)], hidden_result,
        )
        from_b = jnp.concatenate(d, axis=0)
        from_b = from_b.reshape((2, 2, 4) + from_b.shape[1:]).swapaxes(0, 1).reshape(from_b.shape)
        out_part = jnp.concatenate([a[0][:, half // PARTS :], a[1][:, half // PARTS :]], axis=0)
        mine = jnp.concatenate([jnp.concatenate(c, axis=0), from_b, out_part], axis=1)
        other = swap_core(mine)
        shared_out = call_result(
            shared_result(layer), "shared_result", me, layer, [mine, other],
            [(WIDTH, 3 * WIDTH), (WIDTH, WIDTH)], shared_out,
        )

    own = jnp.concatenate([small0[:6], attn_small0[:4], small1[:6], attn_small1[:4]], axis=0)
    send = jnp.concatenate(
        [small0[:4], small0[6:], attn_small0[:4], small1[:4], small1[6:], attn_small1[:4]], axis=0
    )
    sums = sum_small(own, send).reshape(LAYERS, 10, WIDTH)
    attn_bias_grad = jnp.stack([sums[:, 6], sums[:, 7], sums[:, 3]], axis=1)
    norm_gain_grad = jnp.stack([sums[:, 8], sums[:, 1]], axis=1)
    norm_bias_grad = jnp.stack([sums[:, 9], sums[:, 2]], axis=1)
    return (
        output,
        grad0,
        shared_out[0],
        shared_out[1],
        attn_bias_grad,
        norm_gain_grad,
        norm_bias_grad,
        hidden_result[0],
        sums[:, 4:6].reshape(LAYERS, half),
        hidden_result[1],
        sums[:, 0],
    )


def solution(mesh):
    placed = (
        P(("dp", "mp"), None),
        P(("dp", "mp"), None),
        P(("dp", "mp")),
        P(),
        P(),
        P(),
        P(),
        P(),
        P(None, None, "mp"),
        P(None, "mp"),
        P(None, "mp", None),
        P(),
    )
    return jax.shard_map(
        body,
        mesh=mesh,
        in_specs=placed,
        out_specs=(
            P(("dp", "mp"), None),
            P(("dp", "mp"), None),
            P(),
            P(),
            P(),
            P(),
            P(),
            P(None, None, "mp"),
            P(None, "mp"),
            P(None, "mp", None),
            P(),
        ),
        check_vma=False,
    )
```

```python
import jax
import jax.numpy as jnp
import numpy as np
from jax import lax
from jax.experimental import pallas as pl
from jax.experimental.pallas import tpu as pltpu
from jax.sharding import PartitionSpec as P

HEADS = 8
HEAD_DIM = 64
LAYERS = 2
SCHEDULE = (
    "p1 k4 q1 p1", "q1 k5 p0 p1", "q1 p0 k6 q0", "p0 p1 q0 p1",
    "q1 p0 q0 p1", "q0 q1 p0 p1", "q0 p0 q1 q0", "p1 p0 q0 p1",
    "q1 q0 p0 q1", "q0 p0 p1 h10", "q1 s10 h00 h11", "s00 p0 h01 q1",
    "s11 q0 s01",
)
FRAME = 6
SHORT_STEPS = 8
LONG_STEPS = 21
BLK = 128
WIDTH = 512
EPSILON = 1e-05
SCALE = HEAD_DIM ** (-0.5)

ROWS = 512
TURN_ROWS = 256
GROUPS = ROWS // BLK
PAIRS = HEADS // 2
PARTS = 16
COLS = 1024

F32 = jnp.float32
BF16 = jnp.bfloat16
MIB = 1024 * 1024
GRANT = (36, 56)
VMEM = {"attention_forward": 56, "middle_forward": 56, "hidden_turn": 56, "attention_backward": 36, "hidden_backward": 36, "hidden_result": 36, "shared_result": 36}


def mask_bias():
    position = np.arange(BLK)

    def bias(seq_ids, step_ids, valid):
        allowed = (seq_ids[:, None] == seq_ids[None, :]) & (step_ids[None, :] <= step_ids[:, None])
        allowed &= valid[:, None] & valid[None, :]
        return np.where(allowed | np.eye(BLK, dtype=bool), 0.0, -1e30).astype(np.float32)

    short_len = SHORT_STEPS * FRAME
    short = bias(position // short_len, position % short_len // FRAME, position < 2 * short_len)
    long = bias(0 * position, position // FRAME, position < LONG_STEPS * FRAME)
    return np.stack([short, long])


def dot(a, b):
    return jnp.dot(a, b, preferred_element_type=F32)


def dot_nt(a, b):
    return lax.dot_general(a, b, (((1,), (1,)), ((), ())), preferred_element_type=F32)


def dot_tn(a, b):
    return lax.dot_general(a, b, (((0,), (0,)), ((), ())), preferred_element_type=F32)


def normalize(value):
    centered = value - jnp.mean(value, axis=-1, keepdims=True)
    inv_std = lax.rsqrt(jnp.mean(centered * centered, axis=-1, keepdims=True) + EPSILON)
    return centered * inv_std, inv_std


def norm_backward(grad, gain, normal, inv_std):
    scaled = grad * gain
    first = jnp.mean(scaled, axis=-1, keepdims=True)
    second = jnp.mean(scaled * normal, axis=-1, keepdims=True)
    return inv_std * (scaled - first - normal * second)


def column_sum(value):
    return jnp.sum(value, axis=0, keepdims=True)


def add_wide(small, row, value):
    for no in range(value.shape[1] // WIDTH):
        small[row + no : row + no + 1, :] += value[:, no * WIDTH : (no + 1) * WIDTH]


def gelu_parts(pre):
    phi = 0.5 + 0.5 * lax.erf(pre * 0.7071067811865476)
    density = jnp.exp(pre * pre * -0.5) * 0.3989422804014327
    return phi, pre * density


def lane_halves(pair):
    lane = lax.broadcasted_iota(jnp.int32, pair.shape, 1)
    zero = jnp.zeros_like(pair)
    return jnp.concatenate(
        [jnp.where(lane < HEAD_DIM, pair, zero), jnp.where(lane < HEAD_DIM, zero, pair)], axis=0
    )


def attention_forward(stream, layer, step, kinds, mask, qkv_w, out_w, ab, ng, nb, qkv, probs, mixed):
    normal, _ = normalize(stream)
    hidden = (normal * ng[layer, 0:1, :] + nb[layer, 0:1, :]).astype(BF16)
    qkv[:, :WIDTH] = (
        (dot(hidden, qkv_w[:, :WIDTH]) + ab[0, layer : layer + 1, :]) * SCALE
    ).astype(BF16)
    qkv[:, WIDTH : 2 * WIDTH] = dot(hidden, qkv_w[:, WIDTH : 2 * WIDTH]).astype(BF16)
    qkv[:, 2 * WIDTH :] = (dot(hidden, qkv_w[:, 2 * WIDTH :]) + ab[1, layer : layer + 1, :]).astype(BF16)
    groups = stream.shape[0] // BLK
    for group in range(groups):
        rows = slice(group * BLK, (group + 1) * BLK)
        bias = mask[kinds[step * groups + group]]
        for pair in range(PAIRS):
            lanes = slice(pair * BLK, (pair + 1) * BLK)
            keys = lane_halves(qkv[rows, WIDTH + pair * BLK : WIDTH + (pair + 1) * BLK])
            values = lane_halves(qkv[rows, 2 * WIDTH + pair * BLK : 2 * WIDTH + (pair + 1) * BLK])
            scores = dot_nt(qkv[rows, lanes], keys)
            both = []
            for head in range(2):
                part = scores[:, head * BLK : (head + 1) * BLK] + bias
                weights = jnp.exp(part - jnp.max(part, axis=-1, keepdims=True))
                total = jnp.sum(weights, axis=-1, keepdims=True)
                both.append((weights * (1.0 / total)).astype(BF16))
            both = jnp.concatenate(both, axis=1)
            probs[rows, pair * 2 * BLK : (pair + 1) * 2 * BLK] = both
            mixed[rows, lanes] = dot(both, values).astype(BF16)
    return stream + (dot(mixed[...], out_w[...]) + ab[2, layer : layer + 1, :])


def first_kernel(kinds, mask, tokens, qkv_w, out_w, ab, ng, nb, qkv, probs, mixed, middle):
    stream = tokens[...].astype(F32)
    step = pl.program_id(0)
    middle[...] = attention_forward(
        stream, 0, step, kinds, mask, qkv_w, out_w, ab, ng, nb, qkv, probs, mixed
    )


def hidden_blocks(up_own, up_other, down_own, down_other, ub_own, ub_other, layer):
    blocks = []
    for up, down, ub in ((up_own, down_own, ub_own), (up_other, down_other, ub_other)):
        for start in range(0, up.shape[1], COLS):
            cols = slice(start, start + COLS)
            blocks.append((up, down, ub, cols))
    return blocks


def second_kernel(
    kinds, mask, middle, up_own, up_other, down_own, down_other, ub_own, ub_other, db,
    qkv_w, out_w, ab, ng, nb, act, slope, stream_out, qkv, probs, mixed, middle_out,
):
    step = pl.program_id(0)
    value = middle[...]
    normal, _ = normalize(value)
    inner = (normal * ng[0, 1:2, :] + nb[0, 1:2, :]).astype(BF16)
    total = value + db[0:1, :]
    for no, (up, down, ub, cols) in enumerate(
        hidden_blocks(up_own, up_other, down_own, down_other, ub_own, ub_other, 0)
    ):
        pre = dot(inner, up[:, cols]) + ub[0:1, cols]
        phi, tail = gelu_parts(pre)
        active = (pre * phi).astype(BF16)
        act[:, no * COLS : (no + 1) * COLS] = active
        slope[:, no * COLS : (no + 1) * COLS] = (phi + tail).astype(BF16)
        total += dot(active, down[cols, :])
    stream_out[...] = total
    middle_out[...] = attention_forward(
        total, 1, step, kinds, mask, qkv_w, out_w, ab, ng, nb, qkv, probs, mixed
    )


def order_of(core):
    first, second, third, fourth = (0, 1, 2, 3) if core == 0 else (1, 0, 3, 2)
    return [
        (rel >> first & 1) * 8 + (rel >> second & 1) * 4 + (rel >> third & 1) * 2 + (rel >> fourth & 1)
        for rel in range(PARTS)
    ]


def tables(dp, core):
    places = np.array([order_of(0), order_of(1)])
    pieces = np.argsort(places, axis=1)
    mine = np.arange(PARTS)
    rows = [
        np.concatenate(
            [places[c][mine ^ d], places[1 - c][mine ^ d], pieces[c] ^ d, pieces[1 - c] ^ d, [c]]
        )
        for d in range(PARTS)
        for c in range(2)
    ]
    rows = jnp.asarray(np.array(rows, np.int32))
    return lax.dynamic_index_in_dim(rows, (dp & (PARTS - 1)) * 2 + core, keepdims=False)


CORE = 4 * PARTS


def feed_forward_sums(me, gm, act, gpre, inner, mixed, ga, keep, send):
    half = act.shape[1] // 2
    rows_down = half // PARTS
    rows_up = WIDTH // PARTS
    rows_out = WIDTH // 2 // PARTS
    for side, out in enumerate((keep, send)):
        tile = dot_tn(act[:, side * half : (side + 1) * half], gm[...]).astype(BF16)
        for j in range(PARTS):
            place = me[side * PARTS + j]
            out[place, 0:rows_down, :] = tile[j * rows_down : (j + 1) * rows_down]
    for side, out in enumerate((keep, send)):
        tile = dot_tn(inner[...], gpre[:, side * half : (side + 1) * half]).astype(BF16)
        for j in range(PARTS):
            place = me[side * PARTS + j]
            for block in range(half // WIDTH):
                lower = rows_down + block * rows_up
                out[place, lower : lower + rows_up, :] = tile[
                    j * rows_up : (j + 1) * rows_up, block * WIDTH : (block + 1) * WIDTH
                ]
    tile = dot_tn(mixed[...], ga[...]).astype(BF16)
    store_halves(me, tile, 2 * rows_down, rows_out, keep, send)


def store_halves(me, tile, lower, rows, keep, send):
    cut = tile.shape[0] // 2
    straight = me[CORE] == 0
    upper, rest = tile[:cut], tile[cut:]
    for side, out in enumerate((keep, send)):
        value = jnp.where(straight, rest if side else upper, upper if side else rest)
        for j in range(PARTS):
            place = me[side * PARTS + j]
            out[place, lower : lower + rows, :] = value[j * rows : (j + 1) * rows]


def third_kernel(
    me, middle, cot, mixed, up_own, up_other, down_own, down_other, ub_own, ub_other, db, ng, nb,
    output, gmid, keep, send, small,
    act_s, gpre_s, inner_s, gm_s, mixed_s, ga_s,
):
    step = pl.program_id(0)
    count = middle.shape[0]
    rows = pl.ds(pl.multiple_of(step * count, count), count)

    @pl.when(step == 0)
    def _():
        small[...] = jnp.zeros_like(small)

    value = middle[...]
    normal, inv_std = normalize(value)
    inner = (normal * ng[1, 1:2, :] + nb[1, 1:2, :]).astype(BF16)
    inner_s[rows, :] = inner
    gm = cot[...]
    gm_s[rows, :] = gm
    total = value + db[1:2, :]
    ginner = jnp.zeros((count, WIDTH), F32)
    for no, (up, down, ub, cols) in enumerate(
        hidden_blocks(up_own, up_other, down_own, down_other, ub_own, ub_other, 1)
    ):
        pre = dot(inner, up[:, cols]) + ub[1:2, cols]
        phi, tail = gelu_parts(pre)
        active = (pre * phi).astype(BF16)
        act_s[rows, no * COLS : (no + 1) * COLS] = active
        total += dot(active, down[cols, :])
        gpre = (dot_nt(gm, down[cols, :]) * (phi + tail)).astype(BF16)
        gpre_s[rows, no * COLS : (no + 1) * COLS] = gpre
        add_wide(small, 4 + no * (COLS // WIDTH), column_sum(gpre.astype(F32)))
        ginner += dot_nt(gpre, up[:, cols])
    output[...] = total.astype(BF16)
    grad = gm.astype(F32)
    finish_middle(grad, gm, ginner, normal, inv_std, ng[1, 1:2, :], mixed, gmid, small, mixed_s, ga_s, rows)

    @pl.when(step == pl.num_programs(0) - 1)
    def _():
        feed_forward_sums(
            me, gm_s, act_s, gpre_s, inner_s, mixed_s, ga_s, keep, send
        )


def turn_kernel(
    me, kinds, mask, middle, cot, up_own0, up_other0, down_own0, down_other0, qkv_w, out_w,
    up_own1, up_other1, down_own1, down_other1, ub_own, ub_other, db, ab, ng, nb,
    act, slope, stream, qkv, probs, mixed, output, gmid, keep, send, small,
    middle_s, *scratch,
):
    second_kernel(
        kinds, mask, middle, up_own0, up_other0, down_own0, down_other0, ub_own, ub_other, db,
        qkv_w, out_w, ab, ng, nb, act, slope, stream, qkv, probs, mixed, middle_s,
    )
    third_kernel(
        me, middle_s, cot, mixed, up_own1, up_other1, down_own1, down_other1, ub_own, ub_other, db,
        ng, nb, output, gmid, keep, send, small, *scratch,
    )


def finish_middle(grad, gm, ginner, normal, inv_std, gain, mixed, gmid, small, mixed_s, ga_s, rows):
    small[0:1, :] += column_sum(gm.astype(F32))
    small[1:2, :] += column_sum(ginner * normal)
    small[2:3, :] += column_sum(ginner)
    result = grad + norm_backward(ginner, gain, normal, inv_std)
    gmid[...] = result
    ga = result.astype(BF16)
    ga_s[rows, :] = ga
    small[3:4, :] += column_sum(ga.astype(F32))
    mixed_s[rows, :] = mixed[...]


def fifth_kernel(
    me, grad_in, act, slope, middle, mixed, up_own, up_other, down_own, down_other, ng, nb,
    gmid, keep, send, small,
    act_s, gpre_s, inner_s, gm_s, mixed_s, ga_s,
):
    step = pl.program_id(0)
    rows = pl.ds(pl.multiple_of(step * ROWS, ROWS), ROWS)

    @pl.when(step == 0)
    def _():
        small[...] = jnp.zeros_like(small)

    normal, inv_std = normalize(middle[...])
    inner_s[rows, :] = (normal * ng[0, 1:2, :] + nb[0, 1:2, :]).astype(BF16)
    grad = grad_in[...]
    gm = grad.astype(BF16)
    gm_s[rows, :] = gm
    act_s[rows, :] = act[...]
    ginner = jnp.zeros((ROWS, WIDTH), F32)
    for no, (up, down, _, cols) in enumerate(
        hidden_blocks(up_own, up_other, down_own, down_other, None, None, 0)
    ):
        where = slice(no * COLS, (no + 1) * COLS)
        gpre = (dot_nt(gm, down[cols, :]) * slope[:, where].astype(F32)).astype(BF16)
        gpre_s[rows, where] = gpre
        add_wide(small, 4 + no * (COLS // WIDTH), column_sum(gpre.astype(F32)))
        ginner += dot_nt(gpre, up[:, cols])
    finish_middle(grad, gm, ginner, normal, inv_std, ng[0, 1:2, :], mixed, gmid, small, mixed_s, ga_s, rows)

    @pl.when(step == pl.num_programs(0) - 1)
    def _():
        feed_forward_sums(
            me, gm_s, act_s, gpre_s, inner_s, mixed_s, ga_s, keep, send
        )


def attention_backward(layer):
    def kernel(me, gmid, mixed, qkv, probs, stream, qkv_w, out_w, ng, nb, *refs):
        *others, grad_out, keep, send, small, hidden_s, gqkv_s = refs
        step = pl.program_id(0)
        start = pl.multiple_of(step * ROWS, ROWS)

        @pl.when(step == 0)
        def _():
            small[...] = jnp.zeros_like(small)

        gmiddle = gmid[...]
        gmixed = dot_nt(gmiddle.astype(BF16), out_w[...]).astype(BF16)
        product = (gmixed.astype(F32) * mixed[...].astype(F32)).astype(BF16)
        row = lax.broadcasted_iota(jnp.int32, (2 * BLK, BLK), 0)
        lane = lax.broadcasted_iota(jnp.int32, (2 * BLK, BLK), 1)
        minus = jnp.where((row < BLK) == (lane < HEAD_DIM), -1.0, 0.0).astype(BF16)
        for group in range(GROUPS):
            rows = slice(group * BLK, (group + 1) * BLK)
            out_rows = pl.ds(start + group * BLK, BLK)
            lanes = [slice(pair * BLK, (pair + 1) * BLK) for pair in range(PAIRS)]
            k_lanes = [slice(WIDTH + cols.start, WIDTH + cols.stop) for cols in lanes]
            v_lanes = [slice(2 * WIDTH + cols.start, 2 * WIDTH + cols.stop) for cols in lanes]
            gscores = []
            for pair in range(PAIRS):
                left = jnp.concatenate([gmixed[rows, lanes[pair]], product[rows, lanes[pair]]], axis=1)
                right = jnp.concatenate([lane_halves(qkv[rows, v_lanes[pair]]), minus], axis=1)
                gscores.append(dot_nt(left, right))
            for pair in range(PAIRS):
                both = probs[rows, pair * 2 * BLK : (pair + 1) * 2 * BLK]
                tall = jnp.concatenate([both[:, :BLK], both[:, BLK:]], axis=0)
                gvalue = dot_tn(tall, lane_halves(gmixed[rows, lanes[pair]]))
                gqkv_s[out_rows, v_lanes[pair]] = gvalue.astype(BF16)
                gscores[pair] = (both.astype(F32) * gscores[pair]).astype(BF16)
            for pair in range(PAIRS):
                gscore = gscores[pair]
                gquery = dot(gscore, lane_halves(qkv[rows, k_lanes[pair]])) * SCALE
                gqkv_s[out_rows, lanes[pair]] = gquery.astype(BF16)
                tall = jnp.concatenate([gscore[:, :BLK], gscore[:, BLK:]], axis=0)
                gkey = dot_tn(tall, lane_halves(qkv[rows, lanes[pair]]))
                gqkv_s[out_rows, k_lanes[pair]] = gkey.astype(BF16)
        all_rows = pl.ds(start, ROWS)
        gqkv = gqkv_s[all_rows, :]
        small[0:1, :] += column_sum(gqkv[:, :WIDTH].astype(F32))
        small[1:2, :] += column_sum(gqkv[:, 2 * WIDTH :].astype(F32))
        ghidden = dot_nt(gqkv, qkv_w[...])
        normal, inv_std = normalize(stream[...].astype(F32))
        hidden_s[all_rows, :] = (normal * ng[layer, 0:1, :] + nb[layer, 0:1, :]).astype(BF16)
        small[2:3, :] += column_sum(ghidden * normal)
        small[3:4, :] += column_sum(ghidden)
        grad_out[...] = gmiddle + norm_backward(ghidden, ng[layer, 0:1, :], normal, inv_std)

        @pl.when(step == pl.num_programs(0) - 1)
        def _():
            part = WIDTH // 2 // PARTS
            tile = dot_tn(hidden_s[...], gqkv_s[...]).astype(BF16)
            for block in range(3):
                store_halves(
                    me, tile[:, block * WIDTH : (block + 1) * WIDTH], block * part, part, keep, send
                )
            if others:
                small0, small1, attn_small1 = others
                zero = jnp.zeros((part - 2, WIDTH), F32)
                for side, out in enumerate((keep, send)):
                    skip = 4 + 2 * side
                    rows = [
                        small0[0:4, :], small0[skip : skip + 2, :], small[0:4, :],
                        small1[0:4, :], small1[skip : skip + 2, :], attn_small1[0:4, :],
                        jnp.zeros((2 * PARTS - 20, WIDTH), F32),
                    ]
                    rows = jnp.concatenate(rows, axis=0)
                    for j in range(PARTS):
                        piece = jnp.concatenate([rows[2 * j : 2 * j + 2], zero], axis=0)
                        out[me[side * PARTS + j], 3 * part : 4 * part, :] = piece.astype(BF16)

    return kernel


def tiled(width, rows=ROWS):
    return pl.BlockSpec((rows, width), lambda i, *_: (i, 0))


def fixed(*shape):
    return pl.BlockSpec(shape, lambda i, *_: (0,) * len(shape), pipeline_mode=pl.Buffered(1))


def held(*shape):
    return pl.BlockSpec(shape, lambda i, *_: (0,) * len(shape))


def of_layer(layer, *shape):
    return pl.BlockSpec(
        (None,) + shape, lambda i, *_: (layer,) + (0,) * len(shape), pipeline_mode=pl.Buffered(1)
    )


def call(kernel, name, scalar, steps, ins, outs, scratch=(), flops=25 * 10**9, grant=None, **kwargs):
    return pl.pallas_call(
        kernel,
        name=name,
        grid_spec=pltpu.PrefetchScalarGridSpec(
            num_scalar_prefetch=1,
            grid=(steps,),
            in_specs=[spec for _, spec in ins],
            out_specs=[spec for _, _, spec in outs],
            scratch_shapes=list(scratch),
        ),
        out_shape=[jax.ShapeDtypeStruct(shape, dtype) for shape, dtype, _ in outs],
        compiler_params=pltpu.CompilerParams(
            dimension_semantics=("arbitrary",), vmem_limit_bytes=(grant or VMEM[name]) * MIB
        ),
        cost_estimate=pl.CostEstimate(
            flops=flops, bytes_accessed=8 * MIB, transcendentals=0
        ),
        **kwargs,
    )(scalar, *[array for array, _ in ins])


def swap_core(value):
    return lax.ppermute(value, "mp", [(0, 1), (1, 0)])


def swap(value, stage):
    count = lax.axis_size("dp")
    bits = ((1, 2, 4, 8), (2, 1, 8, 4))
    pairs = [
        (2 * i + core, 2 * (i ^ bits[core][stage]) + core) for i in range(count) for core in range(2)
    ]
    return lax.ppermute(value, ("dp", "mp"), pairs)


def add(a, b):
    return (a.astype(F32) + b.astype(F32)).astype(BF16)


def reduce_pieces(keep, send):
    value = add(keep, (yield send, None))
    for stage in range(4):
        cut = value.shape[0] // 2
        value = add(value[:cut], (yield value[cut:], stage))
    bit = PARTS
    while bit < lax.axis_size("dp"):
        pairs = [(i, i ^ bit) for i in range(lax.axis_size("dp"))]
        value = add(value, lax.ppermute(value, "dp", pairs))
        bit *= 2
    for stage in (3, 2, 1):
        value = jnp.concatenate([value, (yield value, stage)], axis=0)
    return (yield value, 0)


class Transfer:
    def __init__(self, stages):
        self.stages = stages
        self.flying = None
        self.sent = None
        self.result = None

    def advance(self, last=()):
        arrived = None
        if self.flying is not None:
            arrived, _ = lax.optimization_barrier((self.flying, last))
        try:
            sent = self.stages.send(arrived)
        except StopIteration as stop:
            self.flying = None
            self.result = stop.value
            return arrived
        self.sent, stage = sent
        self.flying = swap_core(self.sent) if stage is None else swap(self.sent, stage)
        return self.sent


class Job:
    def __init__(self, ref, index, lower, rows, blocks, out, layer, place, half=None, side=0, col=0):
        self.ref, self.index, self.lower = ref, index, lower
        self.rows, self.blocks = rows, blocks
        self.out, self.layer, self.place, self.col = out, layer, place, col
        self.half = half
        self.side = side
        self.shape = (rows, blocks * WIDTH)


def unpack(jobs, shapes, small=None):
    def kernel(me, *refs):
        sems = refs[-1]
        if small:
            rows = refs[-2]
            refs = refs[:-2] + refs[-1:]
        scratch = refs[-len(shapes) - 1 : -1]
        extra = 5 if small else 0
        first = len(refs) - len(shapes) - 3 - extra
        outs = refs[first : first + 2]
        used = dict.fromkeys(shapes, 0)
        copies = []
        for no, job in enumerate(jobs):
            slot = used[job.shape]
            used[job.shape] += 1
            buffer = scratch[list(shapes).index(job.shape)].at[slot]
            source = refs[job.ref].at[job.index]
            for block in range(job.blocks):
                lower = job.lower + block * job.rows
                buffer[:, block * WIDTH : (block + 1) * WIDTH] = source[
                    lower : lower + job.rows, :
                ].astype(F32)
            top = me[(2 + job.side) * PARTS + job.place] * job.rows
            if job.half is not None:
                top += (me[CORE] ^ job.side) * job.half
            where = pl.ds(pl.multiple_of(top, job.rows), job.rows)
            cols = pl.ds(job.col, job.shape[1])
            copy = pltpu.make_async_copy(
                buffer, outs[job.out].at[job.layer, where, cols], sems.at[no]
            )
            copy.start()
            copies.append(copy)
        if small:
            *halves, lower = small
            for place in range(PARTS):
                tile = refs[halves[place // 8]][place % 8, lower : lower + 16, :].astype(F32)
                rows[me[2 * PARTS + place], :, :] = tile[0:8]
            store_small(rows, refs[first + 2 : first + 2 + extra])
        for copy in copies:
            copy.wait()

    return kernel


def store_small(rows, outs):
    attn_bias, norm_gain, norm_bias, up_bias, down_bias = outs

    def row(layer, no):
        no += 10 * layer
        return rows[no // 2, no % 2 : no % 2 + 1, :]

    for layer in range(LAYERS):
        for no, source in enumerate((6, 7, 3)):
            attn_bias[no, layer : layer + 1, :] = row(layer, source)
        for no, source in enumerate((8, 1)):
            norm_gain[layer, no : no + 1, :] = row(layer, source)
        for no, source in enumerate((9, 2)):
            norm_bias[layer, no : no + 1, :] = row(layer, source)
        for no in range(2):
            up_bias[layer : layer + 1, no * WIDTH : (no + 1) * WIDTH] = row(layer, 4 + no)
        down_bias[layer : layer + 1, :] = row(layer, 0)


def call_unpack(name, me, arrays, jobs, shapes, earlier=None, small=None):
    counts = {}
    for job in jobs:
        counts[job.shape] = counts.get(job.shape, 0) + 1
    anywhere = pl.BlockSpec(memory_space=pl.ANY)
    ins = [(array, held(*array.shape)) for array in arrays]
    aliases = {}
    if earlier is not None:
        for no, array in enumerate(earlier):
            aliases[1 + len(ins)] = no
            ins.append((array, anywhere))
    outs = [((LAYERS,) + shape, F32, anywhere) for shape in shapes]
    scratch = [pltpu.VMEM((count,) + shape, F32) for shape, count in counts.items()]
    if small:
        outs += [
            (shape, F32, held(*shape))
            for shape in (
                (3, LAYERS, WIDTH), (LAYERS, 2, WIDTH), (LAYERS, 2, WIDTH),
                (LAYERS, 2 * WIDTH), (LAYERS, WIDTH),
            )
        ]
        scratch.append(pltpu.VMEM((PARTS, 8, WIDTH), F32))
    return call(
        unpack(jobs, counts, small), name, me, 1, ins, outs,
        scratch + [pltpu.SemaphoreType.DMA((len(jobs),))],
        flops=3 * 10**9, input_output_aliases=aliases,
    )


def body(
    tokens, cotangent, block_kinds, qkv_weight, out_weight, attn_bias, norm_gain, norm_bias,
    up_weight, up_bias, down_weight, down_bias,
):
    count = tokens.shape[0]
    steps = count // ROWS
    half = up_weight.shape[2]
    full = 2 * half
    mask = (jnp.asarray(mask_bias()), fixed(2, BLK, BLK))
    me = tables(lax.axis_index("dp"), lax.axis_index("mp"))

    up_other = swap_core(up_weight)
    down_other = swap_core(down_weight)
    ub_other = swap_core(up_bias)

    attn_bias = attn_bias.swapaxes(0, 1)
    ab = (attn_bias, fixed(*attn_bias.shape))
    ng = (norm_gain, fixed(*norm_gain.shape))
    nb = (norm_bias, fixed(*norm_bias.shape))
    db = (down_bias, fixed(*down_bias.shape))
    ubs = [(up_bias, fixed(*up_bias.shape)), (ub_other, fixed(*up_bias.shape))]

    def attention_weights(layer):
        return [
            (qkv_weight, of_layer(layer, WIDTH, 3 * WIDTH)),
            (out_weight, of_layer(layer, WIDTH, WIDTH)),
        ]

    def hidden_weights(layer):
        return [
            (up_weight, of_layer(layer, WIDTH, half)),
            (up_other, of_layer(layer, WIDTH, half)),
            (down_weight, of_layer(layer, half, WIDTH)),
            (down_other, of_layer(layer, half, WIDTH)),
        ]

    def rows_of(width, dtype, rows=ROWS):
        return ((count, width), dtype, tiled(width, rows))

    def blocks(array, rows=ROWS):
        return (array, tiled(array.shape[1], rows))

    attention_outs = [
        rows_of(3 * WIDTH, BF16),
        rows_of(HEADS * BLK, BF16),
        rows_of(WIDTH, BF16),
        rows_of(WIDTH, F32),
    ]

    qkv0, probs0, mixed0, middle0 = call(
        first_kernel, "attention_forward", block_kinds, steps,
        [mask, blocks(tokens)] + attention_weights(0) + [ab, ng, nb],
        attention_outs,
    )
    small_out = ((8, WIDTH), F32, held(8, WIDTH))
    cut = half // PARTS + WIDTH // PARTS * (half // WIDTH)
    part = WIDTH // 2 // PARTS

    def piece_outs(rows):
        return [
            ((PARTS, rows, WIDTH), BF16, pl.BlockSpec((PARTS, rows, WIDTH), lambda i, *_: (0, 0, 0)))
        ] * 2

    hidden_scratch = [
        pltpu.VMEM((count, full), BF16),
        pltpu.VMEM((count, full), BF16),
    ] + [pltpu.VMEM((count, WIDTH), BF16)] * 4

    few = TURN_ROWS
    act0, slope0, stream1, qkv1, probs1, mixed1, output, gmid1, *pieces1, small1 = call(
        turn_kernel, "hidden_turn", me, count // few,
        [(block_kinds, pl.BlockSpec(memory_space=pltpu.SMEM)), mask]
        + [blocks(middle0, few), blocks(cotangent, few)]
        + hidden_weights(0) + attention_weights(1) + hidden_weights(1) + ubs + [db, ab, ng, nb],
        [
            rows_of(full, BF16, few), rows_of(full, BF16, few), rows_of(WIDTH, F32, few),
            rows_of(3 * WIDTH, BF16, few), rows_of(HEADS * BLK, BF16, few), rows_of(WIDTH, BF16, few),
            rows_of(WIDTH, BF16, few), rows_of(WIDTH, F32, few),
        ]
        + piece_outs(cut + part) + [small_out],
        [pltpu.VMEM((few, WIDTH), F32)] + hidden_scratch,
    )

    def attention_back(layer, me, gmid, mixed, qkv, probs, stream, others=()):
        return call(
            attention_backward(layer), "attention_backward", me, steps,
            [blocks(gmid), blocks(mixed), blocks(qkv), blocks(probs), blocks(stream)]
            + attention_weights(layer) + [ng, nb] + [(other, fixed(8, WIDTH)) for other in others],
            [rows_of(WIDTH, F32)] + piece_outs(4 * part if others else 3 * part) + [small_out],
            [pltpu.VMEM((count, WIDTH), BF16), pltpu.VMEM((count, 3 * WIDTH), BF16)],
            grant=GRANT[layer],
        )

    def after(value, last):
        return lax.optimization_barrier((value, last))[0]

    hidden_shapes = [(WIDTH, half), (half, WIDTH)]
    shared_shapes = [(WIDTH, 3 * WIDTH), (WIDTH, WIDTH)]
    halves = (range(8), range(8, 16))

    def hidden_jobs(layer, places):
        jobs = []
        for index, place in enumerate(places):
            jobs.append(Job(0, index, 0, half // PARTS, 1, 1, layer, place))
            jobs.append(
                Job(0, index, half // PARTS, WIDTH // PARTS, half // WIDTH, 0, layer, place)
            )
        return jobs

    def shared_jobs(out, qkv, layer, places, side):
        jobs = []
        for index, place in enumerate(places):
            jobs.append(
                Job(qkv[0], index, qkv[1], part, 3, 0, layer, place, WIDTH // 2, side)
            )
            jobs.append(
                Job(out[0], index, out[1], part, 1, 1, layer, place, WIDTH // 2, side)
            )
        return jobs

    state = {}
    transfers = {}
    results = {"hidden": None, "shared": None}

    def half_of(name, no):
        return transfers[name].result if no else transfers[name].sent

    def hidden_part(layer, no):
        value = after(half_of("p%d" % layer, no), state["last"])
        results["hidden"] = call_unpack(
            "hidden_result", me, [value], hidden_jobs(layer, halves[no]),
            hidden_shapes, results["hidden"],
        )

    def shared_part(layer, no):
        out = after(half_of("p%d" % layer, no), state["last"])
        qkv = half_of("q%d" % layer, no)
        other = swap_core(jnp.concatenate([out[:, cut:], qkv[:, : 3 * part]], axis=1))
        last = layer == 0 and no == 1
        arrays = [out, qkv, other] + ([half_of("q0", 0)] if last else [])
        results["shared"] = call_unpack(
            "shared_result", me, arrays,
            shared_jobs((0, cut), (1, 0), layer, halves[no], 0)
            + shared_jobs((2, 0), (2, part), layer, halves[no], 1),
            shared_shapes, results["shared"], (3, 1, 3 * part) if last else None,
        )

    def join(*values):
        busy = [transfer for transfer in transfers.values() if transfer.flying is not None]
        flying = [transfer.flying for transfer in busy]
        values, flying = lax.optimization_barrier((values, flying))
        for transfer, value in zip(busy, flying):
            transfer.flying = value
        state["last"] = ()
        return values

    def start(name, pieces):
        transfers[name] = Transfer(reduce_pieces(*pieces))

    start("p1", pieces1)
    state["last"] = ()
    for step in " ".join(SCHEDULE).split():
        if step in transfers:
            state["last"] = transfers[step].advance(state["last"])
        elif step == "k4":
            grad1, *pieces, attn_small1 = attention_back(
                1, me, after(gmid1, state["last"]), mixed1, qkv1, probs1, stream1
            )
            grad1, *pieces = join(grad1, *pieces)
            start("q1", pieces)
        elif step == "k5":
            gmid0, *pieces, small0 = call(
                fifth_kernel, "hidden_backward", me, steps,
                [blocks(after(grad1, state["last"])), blocks(act0), blocks(slope0), blocks(middle0), blocks(mixed0)]
                + hidden_weights(0) + [ng, nb],
                [rows_of(WIDTH, F32)] + piece_outs(cut + part) + [small_out],
                hidden_scratch,
            )
            gmid0, *pieces = join(gmid0, *pieces)
            start("p0", pieces)
        elif step == "k6":
            grad0, *pieces, attn_small0 = attention_back(
                0, me, after(gmid0, state["last"]), mixed0, qkv0, probs0, tokens, (small0, small1, attn_small1)
            )
            grad0, *pieces = join(grad0, *pieces)
            start("q0", pieces)
        elif step[0] == "h":
            hidden_part(int(step[1]), int(step[2]))
            state["last"] = results["hidden"]
        else:
            shared_part(int(step[1]), int(step[2]))
            state["last"] = results["shared"]
    hidden_result = results["hidden"]
    shared_out = results["shared"]
    qkv_result, out_result, *small_results = shared_out
    attn_bias_grad, norm_gain_grad, norm_bias_grad, up_bias_grad, down_bias_grad = small_results
    return (
        output,
        grad0,
        qkv_result,
        out_result,
        attn_bias_grad.swapaxes(0, 1),
        norm_gain_grad,
        norm_bias_grad,
        hidden_result[0],
        up_bias_grad,
        hidden_result[1],
        down_bias_grad,
    )


def solution(mesh):
    placed = (
        P(("dp", "mp"), None),
        P(("dp", "mp"), None),
        P(("dp", "mp")),
        P(),
        P(),
        P(),
        P(),
        P(),
        P(None, None, "mp"),
        P(None, "mp"),
        P(None, "mp", None),
        P(),
    )
    return jax.shard_map(
        body,
        mesh=mesh,
        in_specs=placed,
        out_specs=(
            P(("dp", "mp"), None),
            P(("dp", "mp"), None),
            P(),
            P(),
            P(),
            P(),
            P(),
            P(None, None, "mp"),
            P(None, "mp"),
            P(None, "mp", None),
            P(),
        ),
        check_vma=False,
    )
```

```python
import jax
import jax.numpy as jnp
import numpy as np
from jax import lax
from jax.experimental import pallas as pl
from jax.experimental.pallas import tpu as pltpu
from jax.sharding import PartitionSpec as P

HEADS = 8
HEAD_DIM = 64
LAYERS = 2
SCHEDULE = (
    "p1 k4 q1 p1", "q1 k5 p0 p1", "q1 p0 k6 q0", "p0 p1 q0 p1",
    "q1 p0 q0 p1", "q0 q1 p0 p1", "q0 p0 q1 q0", "p1 p0 q0 p1",
    "q1 q0 p0 q1", "q0 p0 p1 h10", "q1 s10 h00 h11", "s00 p0 h01 q1",
    "s11 q0 s01",
)
FRAME = 6
SHORT_STEPS = 8
LONG_STEPS = 21
BLK = 128
WIDTH = 512
EPSILON = 1e-05
SCALE = HEAD_DIM ** (-0.5)

ROWS = 512
TURN_ROWS = 256
GROUPS = ROWS // BLK
PAIRS = HEADS // 2
PARTS = 16
COLS = 1024

F32 = jnp.float32
BF16 = jnp.bfloat16
MIB = 1024 * 1024
GRANT = (36, 56)
VMEM = {"attention_forward": 56, "middle_forward": 56, "hidden_turn": 56, "attention_backward": 36, "hidden_backward": 36, "hidden_result": 36, "shared_result": 36}


def mask_bias():
    position = np.arange(BLK)

    def bias(seq_ids, step_ids, valid):
        allowed = (seq_ids[:, None] == seq_ids[None, :]) & (step_ids[None, :] <= step_ids[:, None])
        allowed &= valid[:, None] & valid[None, :]
        return np.where(allowed | np.eye(BLK, dtype=bool), 0.0, -1e30).astype(np.float32)

    short_len = SHORT_STEPS * FRAME
    short = bias(position // short_len, position % short_len // FRAME, position < 2 * short_len)
    long = bias(0 * position, position // FRAME, position < LONG_STEPS * FRAME)
    return np.stack([short, long])


def dot(a, b):
    return jnp.dot(a, b, preferred_element_type=F32)


def dot_nt(a, b):
    return lax.dot_general(a, b, (((1,), (1,)), ((), ())), preferred_element_type=F32)


def dot_tn(a, b):
    return lax.dot_general(a, b, (((0,), (0,)), ((), ())), preferred_element_type=F32)


def normalize(value):
    centered = value - jnp.mean(value, axis=-1, keepdims=True)
    inv_std = lax.rsqrt(jnp.mean(centered * centered, axis=-1, keepdims=True) + EPSILON)
    return centered * inv_std, inv_std


def norm_backward(grad, gain, normal, inv_std):
    scaled = grad * gain
    first = jnp.mean(scaled, axis=-1, keepdims=True)
    second = jnp.mean(scaled * normal, axis=-1, keepdims=True)
    return inv_std * (scaled - first - normal * second)


def column_sum(value):
    return jnp.sum(value, axis=0, keepdims=True)


def add_wide(small, row, value):
    for no in range(value.shape[1] // WIDTH):
        small[row + no : row + no + 1, :] += value[:, no * WIDTH : (no + 1) * WIDTH]


def gelu_parts(pre):
    phi = 0.5 + 0.5 * lax.erf(pre * 0.7071067811865476)
    density = jnp.exp(pre * pre * -0.5) * 0.3989422804014327
    return phi, pre * density


def lane_halves(pair):
    lane = lax.broadcasted_iota(jnp.int32, pair.shape, 1)
    zero = jnp.zeros_like(pair)
    return jnp.concatenate(
        [jnp.where(lane < HEAD_DIM, pair, zero), jnp.where(lane < HEAD_DIM, zero, pair)], axis=0
    )


def attention_forward(stream, layer, step, kinds, mask, qkv_w, out_w, ab, ng, nb, qkv, probs, mixed):
    normal, _ = normalize(stream)
    hidden = (normal * ng[layer, 0:1, :] + nb[layer, 0:1, :]).astype(BF16)
    qkv[:, :WIDTH] = (
        (dot(hidden, qkv_w[:, :WIDTH]) + ab[0, layer : layer + 1, :]) * SCALE
    ).astype(BF16)
    qkv[:, WIDTH : 2 * WIDTH] = dot(hidden, qkv_w[:, WIDTH : 2 * WIDTH]).astype(BF16)
    qkv[:, 2 * WIDTH :] = (dot(hidden, qkv_w[:, 2 * WIDTH :]) + ab[1, layer : layer + 1, :]).astype(BF16)
    groups = stream.shape[0] // BLK
    for group in range(groups):
        rows = slice(group * BLK, (group + 1) * BLK)
        bias = mask[kinds[step * groups + group]]
        for pair in range(PAIRS):
            lanes = slice(pair * BLK, (pair + 1) * BLK)
            keys = lane_halves(qkv[rows, WIDTH + pair * BLK : WIDTH + (pair + 1) * BLK])
            values = lane_halves(qkv[rows, 2 * WIDTH + pair * BLK : 2 * WIDTH + (pair + 1) * BLK])
            scores = dot_nt(qkv[rows, lanes], keys)
            both = []
            for head in range(2):
                part = scores[:, head * BLK : (head + 1) * BLK] + bias
                weights = jnp.exp(part - jnp.max(part, axis=-1, keepdims=True))
                total = jnp.sum(weights, axis=-1, keepdims=True)
                both.append((weights * (1.0 / total)).astype(BF16))
            both = jnp.concatenate(both, axis=1)
            probs[rows, pair * 2 * BLK : (pair + 1) * 2 * BLK] = both
            mixed[rows, lanes] = dot(both, values).astype(BF16)
    return stream + (dot(mixed[...], out_w[...]) + ab[2, layer : layer + 1, :])


def first_kernel(kinds, mask, tokens, qkv_w, out_w, ab, ng, nb, qkv, probs, mixed, middle):
    stream = tokens[...].astype(F32)
    step = pl.program_id(0)
    middle[...] = attention_forward(
        stream, 0, step, kinds, mask, qkv_w, out_w, ab, ng, nb, qkv, probs, mixed
    )


def hidden_blocks(up_own, up_other, down_own, down_other, ub_own, ub_other, layer):
    blocks = []
    for up, down, ub in ((up_own, down_own, ub_own), (up_other, down_other, ub_other)):
        for start in range(0, up.shape[1], COLS):
            cols = slice(start, start + COLS)
            blocks.append((up, down, ub, cols))
    return blocks


def second_kernel(
    kinds, mask, middle, up_own, up_other, down_own, down_other, ub_own, ub_other, db,
    qkv_w, out_w, ab, ng, nb, act, slope, stream_out, qkv, probs, mixed, middle_out, ready,
):
    step = pl.program_id(0)
    value = middle[...]
    normal, _ = normalize(value)
    inner = (normal * ng[0, 1:2, :] + nb[0, 1:2, :]).astype(BF16)
    total = value + db[0:1, :]
    for no, (up, down, ub, cols) in enumerate(
        hidden_blocks(up_own, up_other, down_own, down_other, ub_own, ub_other, 0)
    ):
        pre = dot(inner, up[:, cols]) + ub[0:1, cols]
        phi, tail = gelu_parts(pre)
        active = (pre * phi).astype(BF16)
        act[:, no * COLS : (no + 1) * COLS] = active
        slope[:, no * COLS : (no + 1) * COLS] = (phi + tail).astype(BF16)
        total += dot(active, down[cols, :])
    stream_out[...] = total
    ready()
    middle_out[...] = attention_forward(
        total, 1, step, kinds, mask, qkv_w, out_w, ab, ng, nb, qkv, probs, mixed
    )


def order_of(core):
    first, second, third, fourth = (0, 1, 2, 3) if core == 0 else (1, 0, 3, 2)
    return [
        (rel >> first & 1) * 8 + (rel >> second & 1) * 4 + (rel >> third & 1) * 2 + (rel >> fourth & 1)
        for rel in range(PARTS)
    ]


def tables(dp, core):
    places = np.array([order_of(0), order_of(1)])
    pieces = np.argsort(places, axis=1)
    mine = np.arange(PARTS)
    rows = [
        np.concatenate(
            [places[c][mine ^ d], places[1 - c][mine ^ d], pieces[c] ^ d, pieces[1 - c] ^ d, [c]]
        )
        for d in range(PARTS)
        for c in range(2)
    ]
    rows = jnp.asarray(np.array(rows, np.int32))
    return lax.dynamic_index_in_dim(rows, (dp & (PARTS - 1)) * 2 + core, keepdims=False)


CORE = 4 * PARTS


def feed_forward_sums(me, gm, act, gpre, inner, mixed, ga, keep, send):
    half = act.shape[1] // 2
    rows_down = half // PARTS
    rows_up = WIDTH // PARTS
    rows_out = WIDTH // 2 // PARTS
    for side, out in enumerate((keep, send)):
        tile = dot_tn(act[:, side * half : (side + 1) * half], gm[...]).astype(BF16)
        for j in range(PARTS):
            place = me[side * PARTS + j]
            out[place, 0:rows_down, :] = tile[j * rows_down : (j + 1) * rows_down]
    for side, out in enumerate((keep, send)):
        tile = dot_tn(inner[...], gpre[:, side * half : (side + 1) * half]).astype(BF16)
        for j in range(PARTS):
            place = me[side * PARTS + j]
            for block in range(half // WIDTH):
                lower = rows_down + block * rows_up
                out[place, lower : lower + rows_up, :] = tile[
                    j * rows_up : (j + 1) * rows_up, block * WIDTH : (block + 1) * WIDTH
                ]
    tile = dot_tn(mixed[...], ga[...]).astype(BF16)
    store_halves(me, tile, 2 * rows_down, rows_out, keep, send)


def store_halves(me, tile, lower, rows, keep, send):
    cut = tile.shape[0] // 2
    straight = me[CORE] == 0
    upper, rest = tile[:cut], tile[cut:]
    for side, out in enumerate((keep, send)):
        value = jnp.where(straight, rest if side else upper, upper if side else rest)
        for j in range(PARTS):
            place = me[side * PARTS + j]
            out[place, lower : lower + rows, :] = value[j * rows : (j + 1) * rows]


def third_kernel(
    me, middle, cot, mixed, up_own, up_other, down_own, down_other, ub_own, ub_other, db, ng, nb,
    output, gmid, keep, send, small,
    act_s, gpre_s, inner_s, gm_s, mixed_s, ga_s,
):
    step = pl.program_id(0)
    count = middle.shape[0]
    rows = pl.ds(pl.multiple_of(step * count, count), count)

    @pl.when(step == 0)
    def _():
        small[...] = jnp.zeros_like(small)

    value = middle[...]
    normal, inv_std = normalize(value)
    inner = (normal * ng[1, 1:2, :] + nb[1, 1:2, :]).astype(BF16)
    inner_s[rows, :] = inner
    gm = cot[...]
    gm_s[rows, :] = gm
    total = value + db[1:2, :]
    ginner = jnp.zeros((count, WIDTH), F32)
    for no, (up, down, ub, cols) in enumerate(
        hidden_blocks(up_own, up_other, down_own, down_other, ub_own, ub_other, 1)
    ):
        pre = dot(inner, up[:, cols]) + ub[1:2, cols]
        phi, tail = gelu_parts(pre)
        active = (pre * phi).astype(BF16)
        act_s[rows, no * COLS : (no + 1) * COLS] = active
        total += dot(active, down[cols, :])
        gpre = (dot_nt(gm, down[cols, :]) * (phi + tail)).astype(BF16)
        gpre_s[rows, no * COLS : (no + 1) * COLS] = gpre
        add_wide(small, 4 + no * (COLS // WIDTH), column_sum(gpre.astype(F32)))
        ginner += dot_nt(gpre, up[:, cols])
    output[...] = total.astype(BF16)
    grad = gm.astype(F32)
    finish_middle(grad, gm, ginner, normal, inv_std, ng[1, 1:2, :], mixed, gmid, small, mixed_s, ga_s, rows)

    @pl.when(step == pl.num_programs(0) - 1)
    def _():
        feed_forward_sums(
            me, gm_s, act_s, gpre_s, inner_s, mixed_s, ga_s, keep, send
        )


def turn_kernel(
    me, kinds, mask, middle, cot, up_own0, up_other0, down_own0, down_other0,
    qkv_all, out_all, up_all, up_other_all, down_all, down_other_all, ub_own, ub_other, db, ab, ng, nb,
    act, slope, stream, qkv, probs, mixed, output, gmid, keep, send, small,
    middle_s, qkv_w, out_w, up_own1, up_other1, down_own1, down_other1, sems, *scratch,
):
    step = pl.program_id(0)
    wholes = (qkv_all, out_all, up_all, up_other_all, down_all, down_other_all)
    buffers = (qkv_w, out_w, up_own1, up_other1, down_own1, down_other1)
    copies = [
        pltpu.make_async_copy(whole.at[1], buffer, sems.at[no])
        for no, (whole, buffer) in enumerate(zip(wholes, buffers))
    ]

    @pl.when(step == 0)
    def _():
        for copy in copies:
            copy.start()

    def arrive(first, last):
        @pl.when(step == 0)
        def _():
            for copy in copies[first:last]:
                copy.wait()

    second_kernel(
        kinds, mask, middle, up_own0, up_other0, down_own0, down_other0, ub_own, ub_other, db,
        qkv_w, out_w, ab, ng, nb, act, slope, stream, qkv, probs, mixed, middle_s,
        lambda: arrive(0, 2),
    )
    arrive(2, 6)
    third_kernel(
        me, middle_s, cot, mixed, up_own1, up_other1, down_own1, down_other1, ub_own, ub_other, db,
        ng, nb, output, gmid, keep, send, small, *scratch,
    )


def finish_middle(grad, gm, ginner, normal, inv_std, gain, mixed, gmid, small, mixed_s, ga_s, rows):
    small[0:1, :] += column_sum(gm.astype(F32))
    small[1:2, :] += column_sum(ginner * normal)
    small[2:3, :] += column_sum(ginner)
    result = grad + norm_backward(ginner, gain, normal, inv_std)
    gmid[...] = result
    ga = result.astype(BF16)
    ga_s[rows, :] = ga
    small[3:4, :] += column_sum(ga.astype(F32))
    mixed_s[rows, :] = mixed[...]


def fifth_kernel(
    me, grad_in, act, slope, middle, mixed, up_own, up_other, down_own, down_other, ng, nb,
    gmid, keep, send, small,
    act_s, gpre_s, inner_s, gm_s, mixed_s, ga_s,
):
    step = pl.program_id(0)
    rows = pl.ds(pl.multiple_of(step * ROWS, ROWS), ROWS)

    @pl.when(step == 0)
    def _():
        small[...] = jnp.zeros_like(small)

    normal, inv_std = normalize(middle[...])
    inner_s[rows, :] = (normal * ng[0, 1:2, :] + nb[0, 1:2, :]).astype(BF16)
    grad = grad_in[...]
    gm = grad.astype(BF16)
    gm_s[rows, :] = gm
    act_s[rows, :] = act[...]
    ginner = jnp.zeros((ROWS, WIDTH), F32)
    for no, (up, down, _, cols) in enumerate(
        hidden_blocks(up_own, up_other, down_own, down_other, None, None, 0)
    ):
        where = slice(no * COLS, (no + 1) * COLS)
        gpre = (dot_nt(gm, down[cols, :]) * slope[:, where].astype(F32)).astype(BF16)
        gpre_s[rows, where] = gpre
        add_wide(small, 4 + no * (COLS // WIDTH), column_sum(gpre.astype(F32)))
        ginner += dot_nt(gpre, up[:, cols])
    finish_middle(grad, gm, ginner, normal, inv_std, ng[0, 1:2, :], mixed, gmid, small, mixed_s, ga_s, rows)

    @pl.when(step == pl.num_programs(0) - 1)
    def _():
        feed_forward_sums(
            me, gm_s, act_s, gpre_s, inner_s, mixed_s, ga_s, keep, send
        )


def attention_backward(layer):
    def kernel(me, gmid, mixed, qkv, probs, stream, qkv_w, out_w, ng, nb, *refs):
        *others, grad_out, keep, send, small, hidden_s, gqkv_s = refs
        step = pl.program_id(0)
        start = pl.multiple_of(step * ROWS, ROWS)

        @pl.when(step == 0)
        def _():
            small[...] = jnp.zeros_like(small)

        gmiddle = gmid[...]
        gmixed = dot_nt(gmiddle.astype(BF16), out_w[...]).astype(BF16)
        product = (gmixed.astype(F32) * mixed[...].astype(F32)).astype(BF16)
        row = lax.broadcasted_iota(jnp.int32, (2 * BLK, BLK), 0)
        lane = lax.broadcasted_iota(jnp.int32, (2 * BLK, BLK), 1)
        minus = jnp.where((row < BLK) == (lane < HEAD_DIM), -1.0, 0.0).astype(BF16)
        for group in range(GROUPS):
            rows = slice(group * BLK, (group + 1) * BLK)
            out_rows = pl.ds(start + group * BLK, BLK)
            lanes = [slice(pair * BLK, (pair + 1) * BLK) for pair in range(PAIRS)]
            k_lanes = [slice(WIDTH + cols.start, WIDTH + cols.stop) for cols in lanes]
            v_lanes = [slice(2 * WIDTH + cols.start, 2 * WIDTH + cols.stop) for cols in lanes]
            gscores = []
            for pair in range(PAIRS):
                left = jnp.concatenate([gmixed[rows, lanes[pair]], product[rows, lanes[pair]]], axis=1)
                right = jnp.concatenate([lane_halves(qkv[rows, v_lanes[pair]]), minus], axis=1)
                gscores.append(dot_nt(left, right))
            for pair in range(PAIRS):
                both = probs[rows, pair * 2 * BLK : (pair + 1) * 2 * BLK]
                tall = jnp.concatenate([both[:, :BLK], both[:, BLK:]], axis=0)
                gvalue = dot_tn(tall, lane_halves(gmixed[rows, lanes[pair]]))
                gqkv_s[out_rows, v_lanes[pair]] = gvalue.astype(BF16)
                gscores[pair] = (both.astype(F32) * gscores[pair]).astype(BF16)
            for pair in range(PAIRS):
                gscore = gscores[pair]
                gquery = dot(gscore, lane_halves(qkv[rows, k_lanes[pair]])) * SCALE
                gqkv_s[out_rows, lanes[pair]] = gquery.astype(BF16)
                tall = jnp.concatenate([gscore[:, :BLK], gscore[:, BLK:]], axis=0)
                gkey = dot_tn(tall, lane_halves(qkv[rows, lanes[pair]]))
                gqkv_s[out_rows, k_lanes[pair]] = gkey.astype(BF16)
        all_rows = pl.ds(start, ROWS)
        gqkv = gqkv_s[all_rows, :]
        small[0:1, :] += column_sum(gqkv[:, :WIDTH].astype(F32))
        small[1:2, :] += column_sum(gqkv[:, 2 * WIDTH :].astype(F32))
        ghidden = dot_nt(gqkv, qkv_w[...])
        normal, inv_std = normalize(stream[...].astype(F32))
        hidden_s[all_rows, :] = (normal * ng[layer, 0:1, :] + nb[layer, 0:1, :]).astype(BF16)
        small[2:3, :] += column_sum(ghidden * normal)
        small[3:4, :] += column_sum(ghidden)
        grad_out[...] = gmiddle + norm_backward(ghidden, ng[layer, 0:1, :], normal, inv_std)

        @pl.when(step == pl.num_programs(0) - 1)
        def _():
            part = WIDTH // 2 // PARTS
            tile = dot_tn(hidden_s[...], gqkv_s[...]).astype(BF16)
            for block in range(3):
                store_halves(
                    me, tile[:, block * WIDTH : (block + 1) * WIDTH], block * part, part, keep, send
                )
            if others:
                small0, small1, attn_small1 = others
                zero = jnp.zeros((part - 2, WIDTH), F32)
                for side, out in enumerate((keep, send)):
                    skip = 4 + 2 * side
                    rows = [
                        small0[0:4, :], small0[skip : skip + 2, :], small[0:4, :],
                        small1[0:4, :], small1[skip : skip + 2, :], attn_small1[0:4, :],
                        jnp.zeros((2 * PARTS - 20, WIDTH), F32),
                    ]
                    rows = jnp.concatenate(rows, axis=0)
                    for j in range(PARTS):
                        piece = jnp.concatenate([rows[2 * j : 2 * j + 2], zero], axis=0)
                        out[me[side * PARTS + j], 3 * part : 4 * part, :] = piece.astype(BF16)

    return kernel


def tiled(width, rows=ROWS):
    return pl.BlockSpec((rows, width), lambda i, *_: (i, 0))


def fixed(*shape):
    return pl.BlockSpec(shape, lambda i, *_: (0,) * len(shape), pipeline_mode=pl.Buffered(1))


def held(*shape):
    return pl.BlockSpec(shape, lambda i, *_: (0,) * len(shape))


def of_layer(layer, *shape):
    return pl.BlockSpec(
        (None,) + shape, lambda i, *_: (layer,) + (0,) * len(shape), pipeline_mode=pl.Buffered(1)
    )


def call(kernel, name, scalar, steps, ins, outs, scratch=(), flops=25 * 10**9, grant=None, **kwargs):
    return pl.pallas_call(
        kernel,
        name=name,
        grid_spec=pltpu.PrefetchScalarGridSpec(
            num_scalar_prefetch=1,
            grid=(steps,),
            in_specs=[spec for _, spec in ins],
            out_specs=[spec for _, _, spec in outs],
            scratch_shapes=list(scratch),
        ),
        out_shape=[jax.ShapeDtypeStruct(shape, dtype) for shape, dtype, _ in outs],
        compiler_params=pltpu.CompilerParams(
            dimension_semantics=("arbitrary",), vmem_limit_bytes=(grant or VMEM[name]) * MIB
        ),
        cost_estimate=pl.CostEstimate(
            flops=flops, bytes_accessed=8 * MIB, transcendentals=0
        ),
        **kwargs,
    )(scalar, *[array for array, _ in ins])


def swap_core(value):
    return lax.ppermute(value, "mp", [(0, 1), (1, 0)])


def swap(value, stage):
    count = lax.axis_size("dp")
    bits = ((1, 2, 4, 8), (2, 1, 8, 4))
    pairs = [
        (2 * i + core, 2 * (i ^ bits[core][stage]) + core) for i in range(count) for core in range(2)
    ]
    return lax.ppermute(value, ("dp", "mp"), pairs)


def add(a, b):
    return (a.astype(F32) + b.astype(F32)).astype(BF16)


def reduce_pieces(keep, send):
    value = add(keep, (yield send, None))
    for stage in range(4):
        cut = value.shape[0] // 2
        value = add(value[:cut], (yield value[cut:], stage))
    bit = PARTS
    while bit < lax.axis_size("dp"):
        pairs = [(i, i ^ bit) for i in range(lax.axis_size("dp"))]
        value = add(value, lax.ppermute(value, "dp", pairs))
        bit *= 2
    for stage in (3, 2, 1):
        value = jnp.concatenate([value, (yield value, stage)], axis=0)
    return (yield value, 0)


class Transfer:
    def __init__(self, stages):
        self.stages = stages
        self.flying = None
        self.sent = None
        self.result = None

    def advance(self, last=()):
        arrived = None
        if self.flying is not None:
            arrived, _ = lax.optimization_barrier((self.flying, last))
        try:
            sent = self.stages.send(arrived)
        except StopIteration as stop:
            self.flying = None
            self.result = stop.value
            return arrived
        self.sent, stage = sent
        self.flying = swap_core(self.sent) if stage is None else swap(self.sent, stage)
        return self.sent


class Job:
    def __init__(self, ref, index, lower, rows, blocks, out, layer, place, half=None, side=0, col=0):
        self.ref, self.index, self.lower = ref, index, lower
        self.rows, self.blocks = rows, blocks
        self.out, self.layer, self.place, self.col = out, layer, place, col
        self.half = half
        self.side = side
        self.shape = (rows, blocks * WIDTH)


def unpack(jobs, shapes, small=None):
    def kernel(me, *refs):
        sems = refs[-1]
        if small:
            rows = refs[-2]
            refs = refs[:-2] + refs[-1:]
        scratch = refs[-len(shapes) - 1 : -1]
        extra = 5 if small else 0
        first = len(refs) - len(shapes) - 3 - extra
        outs = refs[first : first + 2]
        used = dict.fromkeys(shapes, 0)
        copies = []
        for no, job in enumerate(jobs):
            slot = used[job.shape]
            used[job.shape] += 1
            buffer = scratch[list(shapes).index(job.shape)].at[slot]
            source = refs[job.ref].at[job.index]
            for block in range(job.blocks):
                lower = job.lower + block * job.rows
                buffer[:, block * WIDTH : (block + 1) * WIDTH] = source[
                    lower : lower + job.rows, :
                ].astype(F32)
            top = me[(2 + job.side) * PARTS + job.place] * job.rows
            if job.half is not None:
                top += (me[CORE] ^ job.side) * job.half
            where = pl.ds(pl.multiple_of(top, job.rows), job.rows)
            cols = pl.ds(job.col, job.shape[1])
            copy = pltpu.make_async_copy(
                buffer, outs[job.out].at[job.layer, where, cols], sems.at[no]
            )
            copy.start()
            copies.append(copy)
        if small:
            *halves, lower = small
            for place in range(PARTS):
                tile = refs[halves[place // 8]][place % 8, lower : lower + 16, :].astype(F32)
                rows[me[2 * PARTS + place], :, :] = tile[0:8]
            store_small(rows, refs[first + 2 : first + 2 + extra])
        for copy in copies:
            copy.wait()

    return kernel


def store_small(rows, outs):
    attn_bias, norm_gain, norm_bias, up_bias, down_bias = outs

    def row(layer, no):
        no += 10 * layer
        return rows[no // 2, no % 2 : no % 2 + 1, :]

    for layer in range(LAYERS):
        for no, source in enumerate((6, 7, 3)):
            attn_bias[no, layer : layer + 1, :] = row(layer, source)
        for no, source in enumerate((8, 1)):
            norm_gain[layer, no : no + 1, :] = row(layer, source)
        for no, source in enumerate((9, 2)):
            norm_bias[layer, no : no + 1, :] = row(layer, source)
        for no in range(2):
            up_bias[layer : layer + 1, no * WIDTH : (no + 1) * WIDTH] = row(layer, 4 + no)
        down_bias[layer : layer + 1, :] = row(layer, 0)


def call_unpack(name, me, arrays, jobs, shapes, earlier=None, small=None):
    counts = {}
    for job in jobs:
        counts[job.shape] = counts.get(job.shape, 0) + 1
    anywhere = pl.BlockSpec(memory_space=pl.ANY)
    ins = [(array, held(*array.shape)) for array in arrays]
    aliases = {}
    if earlier is not None:
        for no, array in enumerate(earlier):
            aliases[1 + len(ins)] = no
            ins.append((array, anywhere))
    outs = [((LAYERS,) + shape, F32, anywhere) for shape in shapes]
    scratch = [pltpu.VMEM((count,) + shape, F32) for shape, count in counts.items()]
    if small:
        outs += [
            (shape, F32, held(*shape))
            for shape in (
                (3, LAYERS, WIDTH), (LAYERS, 2, WIDTH), (LAYERS, 2, WIDTH),
                (LAYERS, 2 * WIDTH), (LAYERS, WIDTH),
            )
        ]
        scratch.append(pltpu.VMEM((PARTS, 8, WIDTH), F32))
    return call(
        unpack(jobs, counts, small), name, me, 1, ins, outs,
        scratch + [pltpu.SemaphoreType.DMA((len(jobs),))],
        flops=3 * 10**9, input_output_aliases=aliases,
    )


def body(
    tokens, cotangent, block_kinds, qkv_weight, out_weight, attn_bias, norm_gain, norm_bias,
    up_weight, up_bias, down_weight, down_bias,
):
    count = tokens.shape[0]
    steps = count // ROWS
    half = up_weight.shape[2]
    full = 2 * half
    mask = (jnp.asarray(mask_bias()), fixed(2, BLK, BLK))
    me = tables(lax.axis_index("dp"), lax.axis_index("mp"))

    up_other = swap_core(up_weight)
    down_other = swap_core(down_weight)
    ub_other = swap_core(up_bias)

    attn_bias = attn_bias.swapaxes(0, 1)
    ab = (attn_bias, fixed(*attn_bias.shape))
    ng = (norm_gain, fixed(*norm_gain.shape))
    nb = (norm_bias, fixed(*norm_bias.shape))
    db = (down_bias, fixed(*down_bias.shape))
    ubs = [(up_bias, fixed(*up_bias.shape)), (ub_other, fixed(*up_bias.shape))]

    def attention_weights(layer):
        return [
            (qkv_weight, of_layer(layer, WIDTH, 3 * WIDTH)),
            (out_weight, of_layer(layer, WIDTH, WIDTH)),
        ]

    def hidden_weights(layer):
        return [
            (up_weight, of_layer(layer, WIDTH, half)),
            (up_other, of_layer(layer, WIDTH, half)),
            (down_weight, of_layer(layer, half, WIDTH)),
            (down_other, of_layer(layer, half, WIDTH)),
        ]

    def rows_of(width, dtype, rows=ROWS):
        return ((count, width), dtype, tiled(width, rows))

    def blocks(array, rows=ROWS):
        return (array, tiled(array.shape[1], rows))

    attention_outs = [
        rows_of(3 * WIDTH, BF16),
        rows_of(HEADS * BLK, BF16),
        rows_of(WIDTH, BF16),
        rows_of(WIDTH, F32),
    ]

    qkv0, probs0, mixed0, middle0 = call(
        first_kernel, "attention_forward", block_kinds, steps,
        [mask, blocks(tokens)] + attention_weights(0) + [ab, ng, nb],
        attention_outs,
    )
    small_out = ((8, WIDTH), F32, held(8, WIDTH))
    cut = half // PARTS + WIDTH // PARTS * (half // WIDTH)
    part = WIDTH // 2 // PARTS

    def piece_outs(rows):
        return [
            ((PARTS, rows, WIDTH), BF16, pl.BlockSpec((PARTS, rows, WIDTH), lambda i, *_: (0, 0, 0)))
        ] * 2

    hidden_scratch = [
        pltpu.VMEM((count, full), BF16),
        pltpu.VMEM((count, full), BF16),
    ] + [pltpu.VMEM((count, WIDTH), BF16)] * 4

    few = TURN_ROWS
    later = [qkv_weight, out_weight, up_weight, up_other, down_weight, down_other]
    act0, slope0, stream1, qkv1, probs1, mixed1, output, gmid1, *pieces1, small1 = call(
        turn_kernel, "hidden_turn", me, count // few,
        [(block_kinds, pl.BlockSpec(memory_space=pltpu.SMEM)), mask]
        + [blocks(middle0, few), blocks(cotangent, few)]
        + hidden_weights(0) + [(weight, pl.BlockSpec(memory_space=pl.ANY)) for weight in later]
        + ubs + [db, ab, ng, nb],
        [
            rows_of(full, BF16, few), rows_of(full, BF16, few), rows_of(WIDTH, F32, few),
            rows_of(3 * WIDTH, BF16, few), rows_of(HEADS * BLK, BF16, few), rows_of(WIDTH, BF16, few),
            rows_of(WIDTH, BF16, few), rows_of(WIDTH, F32, few),
        ]
        + piece_outs(cut + part) + [small_out],
        [pltpu.VMEM((few, WIDTH), F32)]
        + [pltpu.VMEM(weight.shape[1:], BF16) for weight in later]
        + [pltpu.SemaphoreType.DMA((len(later),))] + hidden_scratch,
    )

    def attention_back(layer, me, gmid, mixed, qkv, probs, stream, others=()):
        return call(
            attention_backward(layer), "attention_backward", me, steps,
            [blocks(gmid), blocks(mixed), blocks(qkv), blocks(probs), blocks(stream)]
            + attention_weights(layer) + [ng, nb] + [(other, fixed(8, WIDTH)) for other in others],
            [rows_of(WIDTH, F32)] + piece_outs(4 * part if others else 3 * part) + [small_out],
            [pltpu.VMEM((count, WIDTH), BF16), pltpu.VMEM((count, 3 * WIDTH), BF16)],
            grant=GRANT[layer],
        )

    def after(value, last):
        return lax.optimization_barrier((value, last))[0]

    hidden_shapes = [(WIDTH, half), (half, WIDTH)]
    shared_shapes = [(WIDTH, 3 * WIDTH), (WIDTH, WIDTH)]
    halves = (range(8), range(8, 16))

    def hidden_jobs(layer, places):
        jobs = []
        for index, place in enumerate(places):
            jobs.append(Job(0, index, 0, half // PARTS, 1, 1, layer, place))
            jobs.append(
                Job(0, index, half // PARTS, WIDTH // PARTS, half // WIDTH, 0, layer, place)
            )
        return jobs

    def shared_jobs(out, qkv, layer, places, side):
        jobs = []
        for index, place in enumerate(places):
            jobs.append(
                Job(qkv[0], index, qkv[1], part, 3, 0, layer, place, WIDTH // 2, side)
            )
            jobs.append(
                Job(out[0], index, out[1], part, 1, 1, layer, place, WIDTH // 2, side)
            )
        return jobs

    state = {}
    transfers = {}
    results = {"hidden": None, "shared": None}

    def half_of(name, no):
        return transfers[name].result if no else transfers[name].sent

    def hidden_part(layer, no):
        value = after(half_of("p%d" % layer, no), state["last"])
        results["hidden"] = call_unpack(
            "hidden_result", me, [value], hidden_jobs(layer, halves[no]),
            hidden_shapes, results["hidden"],
        )

    def shared_part(layer, no):
        out = after(half_of("p%d" % layer, no), state["last"])
        qkv = half_of("q%d" % layer, no)
        other = swap_core(jnp.concatenate([out[:, cut:], qkv[:, : 3 * part]], axis=1))
        last = layer == 0 and no == 1
        arrays = [out, qkv, other] + ([half_of("q0", 0)] if last else [])
        results["shared"] = call_unpack(
            "shared_result", me, arrays,
            shared_jobs((0, cut), (1, 0), layer, halves[no], 0)
            + shared_jobs((2, 0), (2, part), layer, halves[no], 1),
            shared_shapes, results["shared"], (3, 1, 3 * part) if last else None,
        )

    def join(*values, skip=None):
        busy = [
            transfer
            for name, transfer in transfers.items()
            if transfer.flying is not None and name != skip
        ]
        flying = [transfer.flying for transfer in busy]
        values, flying = lax.optimization_barrier((values, flying))
        for transfer, value in zip(busy, flying):
            transfer.flying = value
        state["last"] = ()
        return values

    def start(name, pieces):
        transfers[name] = Transfer(reduce_pieces(*pieces))

    start("p1", pieces1)
    state["last"] = ()
    for step in " ".join(SCHEDULE).split():
        if step in transfers:
            state["last"] = transfers[step].advance(state["last"])
        elif step == "k4":
            grad1, *pieces, attn_small1 = attention_back(
                1, me, after(gmid1, state["last"]), mixed1, qkv1, probs1, stream1
            )
            grad1, *pieces = join(grad1, *pieces)
            start("q1", pieces)
        elif step == "k5":
            gmid0, *pieces, small0 = call(
                fifth_kernel, "hidden_backward", me, steps,
                [blocks(after(grad1, state["last"])), blocks(act0), blocks(slope0), blocks(middle0), blocks(mixed0)]
                + hidden_weights(0) + [ng, nb],
                [rows_of(WIDTH, F32)] + piece_outs(cut + part) + [small_out],
                hidden_scratch,
            )
            gmid0, *pieces = join(gmid0, *pieces)
            start("p0", pieces)
        elif step == "k6":
            grad0, *pieces, attn_small0 = attention_back(
                0, me, after(gmid0, state["last"]), mixed0, qkv0, probs0, tokens, (small0, small1, attn_small1)
            )
            grad0, *pieces = join(grad0, *pieces, skip="p0")
            start("q0", pieces)
        elif step[0] == "h":
            hidden_part(int(step[1]), int(step[2]))
            state["last"] = results["hidden"]
        else:
            shared_part(int(step[1]), int(step[2]))
            state["last"] = results["shared"]
    hidden_result = results["hidden"]
    shared_out = results["shared"]
    qkv_result, out_result, *small_results = shared_out
    attn_bias_grad, norm_gain_grad, norm_bias_grad, up_bias_grad, down_bias_grad = small_results
    return (
        output,
        grad0,
        qkv_result,
        out_result,
        attn_bias_grad.swapaxes(0, 1),
        norm_gain_grad,
        norm_bias_grad,
        hidden_result[0],
        up_bias_grad,
        hidden_result[1],
        down_bias_grad,
    )


def solution(mesh):
    placed = (
        P(("dp", "mp"), None),
        P(("dp", "mp"), None),
        P(("dp", "mp")),
        P(),
        P(),
        P(),
        P(),
        P(),
        P(None, None, "mp"),
        P(None, "mp"),
        P(None, "mp", None),
        P(),
    )
    return jax.shard_map(
        body,
        mesh=mesh,
        in_specs=placed,
        out_specs=(
            P(("dp", "mp"), None),
            P(("dp", "mp"), None),
            P(),
            P(),
            P(),
            P(),
            P(),
            P(None, None, "mp"),
            P(None, "mp"),
            P(None, "mp", None),
            P(),
        ),
        check_vma=False,
    )
```

```python
import jax
import jax.numpy as jnp
import numpy as np
from jax import lax
from jax.experimental import pallas as pl
from jax.experimental.pallas import tpu as pltpu
from jax.sharding import PartitionSpec as P

HEADS = 8
HEAD_DIM = 64
LAYERS = 2
SCHEDULE = (
    "p1 k4 q1 p1", "q1 k5 p0 p1", "q1 p0 k6 q0", "p0 p1 q0 p1",
    "q1 p0 q0 p1", "q0 q1 p0 p1", "q0 p0 q1 q0", "p1 p0 q0 p1",
    "q1 q0 p0 q1", "q0 p0 p1 h10", "q1 s10 h00 h11", "s00 p0 h01 q1",
    "s11 q0 s01",
)
FRAME = 6
SHORT_STEPS = 8
LONG_STEPS = 21
BLK = 128
WIDTH = 512
EPSILON = 1e-05
SCALE = HEAD_DIM ** (-0.5)

ROWS = 512
TURN_ROWS = 256
GROUPS = ROWS // BLK
PAIRS = HEADS // 2
PARTS = 16
COLS = 1024

F32 = jnp.float32
BF16 = jnp.bfloat16
MIB = 1024 * 1024
GRANT = (36, 56)
VMEM = {"attention_forward": 56, "middle_forward": 56, "hidden_turn": 56, "attention_backward": 36, "hidden_backward": 36, "hidden_result": 36, "shared_result": 36}


def mask_bias():
    position = np.arange(BLK)

    def bias(seq_ids, step_ids, valid):
        allowed = (seq_ids[:, None] == seq_ids[None, :]) & (step_ids[None, :] <= step_ids[:, None])
        allowed &= valid[:, None] & valid[None, :]
        return np.where(allowed | np.eye(BLK, dtype=bool), 0.0, -1e30).astype(np.float32)

    short_len = SHORT_STEPS * FRAME
    short = bias(position // short_len, position % short_len // FRAME, position < 2 * short_len)
    long = bias(0 * position, position // FRAME, position < LONG_STEPS * FRAME)
    return np.stack([short, long])


def dot(a, b):
    return jnp.dot(a, b, preferred_element_type=F32)


def dot_nt(a, b):
    return lax.dot_general(a, b, (((1,), (1,)), ((), ())), preferred_element_type=F32)


def dot_tn(a, b):
    return lax.dot_general(a, b, (((0,), (0,)), ((), ())), preferred_element_type=F32)


def normalize(value):
    centered = value - jnp.mean(value, axis=-1, keepdims=True)
    inv_std = lax.rsqrt(jnp.mean(centered * centered, axis=-1, keepdims=True) + EPSILON)
    return centered * inv_std, inv_std


def norm_backward(grad, gain, normal, inv_std):
    scaled = grad * gain
    first = jnp.mean(scaled, axis=-1, keepdims=True)
    second = jnp.mean(scaled * normal, axis=-1, keepdims=True)
    return inv_std * (scaled - first - normal * second)


def column_sum(value):
    return jnp.sum(value, axis=0, keepdims=True)


def add_wide(small, row, value):
    for no in range(value.shape[1] // WIDTH):
        small[row + no : row + no + 1, :] += value[:, no * WIDTH : (no + 1) * WIDTH]


def gelu_parts(pre):
    phi = 0.5 + 0.5 * lax.erf(pre * 0.7071067811865476)
    density = jnp.exp(pre * pre * -0.5) * 0.3989422804014327
    return phi, pre * density


def lane_halves(pair):
    lane = lax.broadcasted_iota(jnp.int32, pair.shape, 1)
    zero = jnp.zeros_like(pair)
    return jnp.concatenate(
        [jnp.where(lane < HEAD_DIM, pair, zero), jnp.where(lane < HEAD_DIM, zero, pair)], axis=0
    )


def attention_forward(stream, layer, step, kinds, mask, qkv_w, out_w, ab, ng, nb, qkv, probs, mixed):
    normal, _ = normalize(stream)
    hidden = (normal * ng[layer, 0:1, :] + nb[layer, 0:1, :]).astype(BF16)
    qkv[:, :WIDTH] = (
        (dot(hidden, qkv_w[:, :WIDTH]) + ab[0, layer : layer + 1, :]) * SCALE
    ).astype(BF16)
    qkv[:, WIDTH : 2 * WIDTH] = dot(hidden, qkv_w[:, WIDTH : 2 * WIDTH]).astype(BF16)
    qkv[:, 2 * WIDTH :] = (dot(hidden, qkv_w[:, 2 * WIDTH :]) + ab[1, layer : layer + 1, :]).astype(BF16)
    groups = stream.shape[0] // BLK
    for group in range(groups):
        rows = slice(group * BLK, (group + 1) * BLK)
        bias = mask[kinds[step * groups + group]]
        for pair in range(PAIRS):
            lanes = slice(pair * BLK, (pair + 1) * BLK)
            keys = lane_halves(qkv[rows, WIDTH + pair * BLK : WIDTH + (pair + 1) * BLK])
            values = lane_halves(qkv[rows, 2 * WIDTH + pair * BLK : 2 * WIDTH + (pair + 1) * BLK])
            scores = dot_nt(qkv[rows, lanes], keys)
            both = []
            for head in range(2):
                part = scores[:, head * BLK : (head + 1) * BLK] + bias
                weights = jnp.exp(part - jnp.max(part, axis=-1, keepdims=True))
                total = jnp.sum(weights, axis=-1, keepdims=True)
                both.append((weights * (1.0 / total)).astype(BF16))
            both = jnp.concatenate(both, axis=1)
            probs[rows, pair * 2 * BLK : (pair + 1) * 2 * BLK] = both
            mixed[rows, lanes] = dot(both, values).astype(BF16)
    return stream + (dot(mixed[...], out_w[...]) + ab[2, layer : layer + 1, :])


def first_kernel(kinds, mask, tokens, qkv_w, out_w, ab, ng, nb, qkv, probs, mixed, middle):
    stream = tokens[...].astype(F32)
    step = pl.program_id(0)
    middle[...] = attention_forward(
        stream, 0, step, kinds, mask, qkv_w, out_w, ab, ng, nb, qkv, probs, mixed
    )


def hidden_blocks(up_own, up_other, down_own, down_other, ub_own, ub_other, layer):
    blocks = []
    for up, down, ub in ((up_own, down_own, ub_own), (up_other, down_other, ub_other)):
        for start in range(0, up.shape[1], COLS):
            cols = slice(start, start + COLS)
            blocks.append((up, down, ub, cols))
    return blocks


def second_kernel(
    kinds, mask, middle, up_own, up_other, down_own, down_other, ub_own, ub_other, db,
    qkv_w, out_w, ab, ng, nb, act, slope, stream_out, qkv, probs, mixed, middle_out, ready,
):
    step = pl.program_id(0)
    value = middle[...]
    normal, _ = normalize(value)
    inner = (normal * ng[0, 1:2, :] + nb[0, 1:2, :]).astype(BF16)
    total = value + db[0:1, :]
    for no, (up, down, ub, cols) in enumerate(
        hidden_blocks(up_own, up_other, down_own, down_other, ub_own, ub_other, 0)
    ):
        pre = dot(inner, up[:, cols]) + ub[0:1, cols]
        phi, tail = gelu_parts(pre)
        active = (pre * phi).astype(BF16)
        act[:, no * COLS : (no + 1) * COLS] = active
        slope[:, no * COLS : (no + 1) * COLS] = (phi + tail).astype(BF16)
        total += dot(active, down[cols, :])
    stream_out[...] = total
    ready()
    middle_out[...] = attention_forward(
        total, 1, step, kinds, mask, qkv_w, out_w, ab, ng, nb, qkv, probs, mixed
    )


def order_of(core):
    first, second, third, fourth = (0, 1, 2, 3) if core == 0 else (1, 0, 3, 2)
    return [
        (rel >> first & 1) * 8 + (rel >> second & 1) * 4 + (rel >> third & 1) * 2 + (rel >> fourth & 1)
        for rel in range(PARTS)
    ]


def tables(dp, core):
    places = np.array([order_of(0), order_of(1)])
    pieces = np.argsort(places, axis=1)
    mine = np.arange(PARTS)
    rows = [
        np.concatenate(
            [places[c][mine ^ d], places[1 - c][mine ^ d], pieces[c] ^ d, pieces[1 - c] ^ d, [c]]
        )
        for d in range(PARTS)
        for c in range(2)
    ]
    rows = jnp.asarray(np.array(rows, np.int32))
    return lax.dynamic_index_in_dim(rows, (dp & (PARTS - 1)) * 2 + core, keepdims=False)


CORE = 4 * PARTS


def feed_forward_sums(me, gm, act, gpre, inner, mixed, ga, keep, send):
    half = act.shape[1] // 2
    rows_down = half // PARTS
    rows_up = WIDTH // PARTS
    rows_out = WIDTH // 2 // PARTS
    for side, out in enumerate((keep, send)):
        tile = dot_tn(act[:, side * half : (side + 1) * half], gm[...]).astype(BF16)
        for j in range(PARTS):
            place = me[side * PARTS + j]
            out[place, 0:rows_down, :] = tile[j * rows_down : (j + 1) * rows_down]
    for side, out in enumerate((keep, send)):
        tile = dot_tn(inner[...], gpre[:, side * half : (side + 1) * half]).astype(BF16)
        for j in range(PARTS):
            place = me[side * PARTS + j]
            for block in range(half // WIDTH):
                lower = rows_down + block * rows_up
                out[place, lower : lower + rows_up, :] = tile[
                    j * rows_up : (j + 1) * rows_up, block * WIDTH : (block + 1) * WIDTH
                ]
    tile = dot_tn(mixed[...], ga[...]).astype(BF16)
    store_halves(me, tile, 2 * rows_down, rows_out, keep, send)


def store_halves(me, tile, lower, rows, keep, send):
    cut = tile.shape[0] // 2
    straight = me[CORE] == 0
    upper, rest = tile[:cut], tile[cut:]
    for side, out in enumerate((keep, send)):
        value = jnp.where(straight, rest if side else upper, upper if side else rest)
        for j in range(PARTS):
            place = me[side * PARTS + j]
            out[place, lower : lower + rows, :] = value[j * rows : (j + 1) * rows]


def third_kernel(
    me, middle, cot, mixed, up_own, up_other, down_own, down_other, ub_own, ub_other, db, ng, nb,
    output, gmid, keep, send, small,
    act_s, gpre_s, inner_s, gm_s, mixed_s, ga_s,
):
    step = pl.program_id(0)
    count = middle.shape[0]
    rows = pl.ds(pl.multiple_of(step * count, count), count)

    @pl.when(step == 0)
    def _():
        small[...] = jnp.zeros_like(small)

    value = middle[...]
    normal, inv_std = normalize(value)
    inner = (normal * ng[1, 1:2, :] + nb[1, 1:2, :]).astype(BF16)
    inner_s[rows, :] = inner
    gm = cot[...]
    gm_s[rows, :] = gm
    total = value + db[1:2, :]
    ginner = jnp.zeros((count, WIDTH), F32)
    for no, (up, down, ub, cols) in enumerate(
        hidden_blocks(up_own, up_other, down_own, down_other, ub_own, ub_other, 1)
    ):
        pre = dot(inner, up[:, cols]) + ub[1:2, cols]
        phi, tail = gelu_parts(pre)
        active = (pre * phi).astype(BF16)
        act_s[rows, no * COLS : (no + 1) * COLS] = active
        total += dot(active, down[cols, :])
        gpre = (dot_nt(gm, down[cols, :]) * (phi + tail)).astype(BF16)
        gpre_s[rows, no * COLS : (no + 1) * COLS] = gpre
        add_wide(small, 4 + no * (COLS // WIDTH), column_sum(gpre.astype(F32)))
        ginner += dot_nt(gpre, up[:, cols])
    output[...] = total.astype(BF16)
    grad = gm.astype(F32)
    finish_middle(grad, gm, ginner, normal, inv_std, ng[1, 1:2, :], mixed, gmid, small, mixed_s, ga_s, rows)

    @pl.when(step == pl.num_programs(0) - 1)
    def _():
        feed_forward_sums(
            me, gm_s, act_s, gpre_s, inner_s, mixed_s, ga_s, keep, send
        )


def turn_kernel(
    me, kinds, mask, middle, cot, up_own0, up_other0, down_own0, down_other0,
    qkv_all, out_all, up_all, up_other_all, down_all, down_other_all, ub_own, ub_other, db, ab, ng, nb,
    act, slope, stream, qkv, probs, mixed, output, gmid, keep, send, small,
    middle_s, qkv_w, out_w, up_own1, up_other1, down_own1, down_other1, sems, *scratch,
):
    step = pl.program_id(0)
    wholes = (qkv_all, out_all, up_all, up_other_all, down_all, down_other_all)
    buffers = (qkv_w, out_w, up_own1, up_other1, down_own1, down_other1)
    copies = [
        pltpu.make_async_copy(whole.at[1], buffer, sems.at[no])
        for no, (whole, buffer) in enumerate(zip(wholes, buffers))
    ]

    @pl.when(step == 0)
    def _():
        for copy in copies:
            copy.start()

    def arrive(first, last):
        @pl.when(step == 0)
        def _():
            for copy in copies[first:last]:
                copy.wait()

    second_kernel(
        kinds, mask, middle, up_own0, up_other0, down_own0, down_other0, ub_own, ub_other, db,
        qkv_w, out_w, ab, ng, nb, act, slope, stream, qkv, probs, mixed, middle_s,
        lambda: arrive(0, 2),
    )
    arrive(2, 6)
    third_kernel(
        me, middle_s, cot, mixed, up_own1, up_other1, down_own1, down_other1, ub_own, ub_other, db,
        ng, nb, output, gmid, keep, send, small, *scratch,
    )


def finish_middle(grad, gm, ginner, normal, inv_std, gain, mixed, gmid, small, mixed_s, ga_s, rows):
    small[0:1, :] += column_sum(gm.astype(F32))
    small[1:2, :] += column_sum(ginner * normal)
    small[2:3, :] += column_sum(ginner)
    result = grad + norm_backward(ginner, gain, normal, inv_std)
    gmid[...] = result
    ga = result.astype(BF16)
    ga_s[rows, :] = ga
    small[3:4, :] += column_sum(ga.astype(F32))
    mixed_s[rows, :] = mixed[...]


def fifth_kernel(
    me, grad_in, act, slope, middle, mixed, up_own, up_other, down_own, down_other, ng, nb,
    gmid, keep, send, small,
    act_s, gpre_s, inner_s, gm_s, mixed_s, ga_s,
):
    step = pl.program_id(0)
    rows = pl.ds(pl.multiple_of(step * ROWS, ROWS), ROWS)

    @pl.when(step == 0)
    def _():
        small[...] = jnp.zeros_like(small)

    normal, inv_std = normalize(middle[...])
    inner_s[rows, :] = (normal * ng[0, 1:2, :] + nb[0, 1:2, :]).astype(BF16)
    grad = grad_in[...]
    gm = grad.astype(BF16)
    gm_s[rows, :] = gm
    act_s[rows, :] = act[...]
    ginner = jnp.zeros((ROWS, WIDTH), F32)
    for no, (up, down, _, cols) in enumerate(
        hidden_blocks(up_own, up_other, down_own, down_other, None, None, 0)
    ):
        where = slice(no * COLS, (no + 1) * COLS)
        gpre = (dot_nt(gm, down[cols, :]) * slope[:, where].astype(F32)).astype(BF16)
        gpre_s[rows, where] = gpre
        add_wide(small, 4 + no * (COLS // WIDTH), column_sum(gpre.astype(F32)))
        ginner += dot_nt(gpre, up[:, cols])
    finish_middle(grad, gm, ginner, normal, inv_std, ng[0, 1:2, :], mixed, gmid, small, mixed_s, ga_s, rows)

    @pl.when(step == pl.num_programs(0) - 1)
    def _():
        feed_forward_sums(
            me, gm_s, act_s, gpre_s, inner_s, mixed_s, ga_s, keep, send
        )


def attention_backward(layer):
    def kernel(me, gmid, mixed, qkv, probs, stream, qkv_w, out_w, ng, nb, *refs):
        *others, grad_out, keep, send, small, hidden_s, gqkv_s = refs
        step = pl.program_id(0)
        start = pl.multiple_of(step * ROWS, ROWS)

        @pl.when(step == 0)
        def _():
            small[...] = jnp.zeros_like(small)

        gmiddle = gmid[...]
        gmixed = dot_nt(gmiddle.astype(BF16), out_w[...]).astype(BF16)
        product = (gmixed.astype(F32) * mixed[...].astype(F32)).astype(BF16)
        row = lax.broadcasted_iota(jnp.int32, (2 * BLK, BLK), 0)
        lane = lax.broadcasted_iota(jnp.int32, (2 * BLK, BLK), 1)
        minus = jnp.where((row < BLK) == (lane < HEAD_DIM), -1.0, 0.0).astype(BF16)
        for group in range(GROUPS):
            rows = slice(group * BLK, (group + 1) * BLK)
            out_rows = pl.ds(start + group * BLK, BLK)
            lanes = [slice(pair * BLK, (pair + 1) * BLK) for pair in range(PAIRS)]
            k_lanes = [slice(WIDTH + cols.start, WIDTH + cols.stop) for cols in lanes]
            v_lanes = [slice(2 * WIDTH + cols.start, 2 * WIDTH + cols.stop) for cols in lanes]
            gscores = []
            for pair in range(PAIRS):
                left = jnp.concatenate([gmixed[rows, lanes[pair]], product[rows, lanes[pair]]], axis=1)
                right = jnp.concatenate([lane_halves(qkv[rows, v_lanes[pair]]), minus], axis=1)
                gscores.append(dot_nt(left, right))
            for pair in range(PAIRS):
                both = probs[rows, pair * 2 * BLK : (pair + 1) * 2 * BLK]
                tall = jnp.concatenate([both[:, :BLK], both[:, BLK:]], axis=0)
                gvalue = dot_tn(tall, lane_halves(gmixed[rows, lanes[pair]]))
                gqkv_s[out_rows, v_lanes[pair]] = gvalue.astype(BF16)
                gscores[pair] = (both.astype(F32) * gscores[pair]).astype(BF16)
            for pair in range(PAIRS):
                gscore = gscores[pair]
                gquery = dot(gscore, lane_halves(qkv[rows, k_lanes[pair]])) * SCALE
                gqkv_s[out_rows, lanes[pair]] = gquery.astype(BF16)
                tall = jnp.concatenate([gscore[:, :BLK], gscore[:, BLK:]], axis=0)
                gkey = dot_tn(tall, lane_halves(qkv[rows, lanes[pair]]))
                gqkv_s[out_rows, k_lanes[pair]] = gkey.astype(BF16)
        all_rows = pl.ds(start, ROWS)
        gqkv = gqkv_s[all_rows, :]
        small[0:1, :] += column_sum(gqkv[:, :WIDTH].astype(F32))
        small[1:2, :] += column_sum(gqkv[:, 2 * WIDTH :].astype(F32))
        ghidden = dot_nt(gqkv, qkv_w[...])
        normal, inv_std = normalize(stream[...].astype(F32))
        hidden_s[all_rows, :] = (normal * ng[layer, 0:1, :] + nb[layer, 0:1, :]).astype(BF16)
        small[2:3, :] += column_sum(ghidden * normal)
        small[3:4, :] += column_sum(ghidden)
        grad_out[...] = gmiddle + norm_backward(ghidden, ng[layer, 0:1, :], normal, inv_std)

        @pl.when(step == pl.num_programs(0) - 1)
        def _():
            part = WIDTH // 2 // PARTS
            tile = dot_tn(hidden_s[...], gqkv_s[...]).astype(BF16)
            for block in range(3):
                store_halves(
                    me, tile[:, block * WIDTH : (block + 1) * WIDTH], block * part, part, keep, send
                )
            if others:
                small0, small1, attn_small1 = others
                zero = jnp.zeros((part - 2, WIDTH), F32)
                for side, out in enumerate((keep, send)):
                    skip = 4 + 2 * side
                    rows = [
                        small0[0:4, :], small0[skip : skip + 2, :], small[0:4, :],
                        small1[0:4, :], small1[skip : skip + 2, :], attn_small1[0:4, :],
                        jnp.zeros((2 * PARTS - 20, WIDTH), F32),
                    ]
                    rows = jnp.concatenate(rows, axis=0)
                    for j in range(PARTS):
                        piece = jnp.concatenate([rows[2 * j : 2 * j + 2], zero], axis=0)
                        out[me[side * PARTS + j], 3 * part : 4 * part, :] = piece.astype(BF16)

    return kernel


def tiled(width, rows=ROWS):
    return pl.BlockSpec((rows, width), lambda i, *_: (i, 0))


def fixed(*shape):
    return pl.BlockSpec(shape, lambda i, *_: (0,) * len(shape), pipeline_mode=pl.Buffered(1))


def held(*shape):
    return pl.BlockSpec(shape, lambda i, *_: (0,) * len(shape))


def of_layer(layer, *shape):
    return pl.BlockSpec(
        (None,) + shape, lambda i, *_: (layer,) + (0,) * len(shape), pipeline_mode=pl.Buffered(1)
    )


def call(kernel, name, scalar, steps, ins, outs, scratch=(), flops=25 * 10**9, grant=None, **kwargs):
    return pl.pallas_call(
        kernel,
        name=name,
        grid_spec=pltpu.PrefetchScalarGridSpec(
            num_scalar_prefetch=1,
            grid=(steps,),
            in_specs=[spec for _, spec in ins],
            out_specs=[spec for _, _, spec in outs],
            scratch_shapes=list(scratch),
        ),
        out_shape=[jax.ShapeDtypeStruct(shape, dtype) for shape, dtype, _ in outs],
        compiler_params=pltpu.CompilerParams(
            dimension_semantics=("arbitrary",), vmem_limit_bytes=(grant or VMEM[name]) * MIB
        ),
        cost_estimate=pl.CostEstimate(
            flops=flops, bytes_accessed=8 * MIB, transcendentals=0
        ),
        **kwargs,
    )(scalar, *[array for array, _ in ins])


def swap_core(value):
    return lax.ppermute(value, "mp", [(0, 1), (1, 0)])


def swap(value, stage):
    count = lax.axis_size("dp")
    bits = ((1, 2, 4, 8), (2, 1, 8, 4))
    pairs = [
        (2 * i + core, 2 * (i ^ bits[core][stage]) + core) for i in range(count) for core in range(2)
    ]
    return lax.ppermute(value, ("dp", "mp"), pairs)


def add(a, b):
    return (a.astype(F32) + b.astype(F32)).astype(BF16)


def reduce_pieces(keep, send):
    value = add(keep, (yield send, None))
    for stage in range(4):
        cut = value.shape[0] // 2
        value = add(value[:cut], (yield value[cut:], stage))
    bit = PARTS
    while bit < lax.axis_size("dp"):
        pairs = [(i, i ^ bit) for i in range(lax.axis_size("dp"))]
        value = add(value, lax.ppermute(value, "dp", pairs))
        bit *= 2
    for stage in (3, 2, 1):
        value = jnp.concatenate([value, (yield value, stage)], axis=0)
    return (yield value, 0)


class Transfer:
    def __init__(self, stages):
        self.stages = stages
        self.flying = None
        self.sent = None
        self.result = None

    def advance(self, last=()):
        arrived = None
        if self.flying is not None:
            arrived, _ = lax.optimization_barrier((self.flying, last))
        try:
            sent = self.stages.send(arrived)
        except StopIteration as stop:
            self.flying = None
            self.result = stop.value
            return arrived
        self.sent, stage = sent
        self.flying = swap_core(self.sent) if stage is None else swap(self.sent, stage)
        return self.sent


class Job:
    def __init__(self, ref, index, lower, rows, blocks, out, layer, place, half=None, side=0, col=0):
        self.ref, self.index, self.lower = ref, index, lower
        self.rows, self.blocks = rows, blocks
        self.out, self.layer, self.place, self.col = out, layer, place, col
        self.half = half
        self.side = side
        self.shape = (rows, blocks * WIDTH)


def unpack(jobs, shapes, small=None):
    def kernel(me, *refs):
        sems = refs[-1]
        if small:
            rows = refs[-2]
            refs = refs[:-2] + refs[-1:]
        scratch = refs[-len(shapes) - 1 : -1]
        extra = 5 if small else 0
        first = len(refs) - len(shapes) - 3 - extra
        outs = refs[first : first + 2]
        used = dict.fromkeys(shapes, 0)
        copies = []
        for no, job in enumerate(jobs):
            slot = used[job.shape]
            used[job.shape] += 1
            buffer = scratch[list(shapes).index(job.shape)].at[slot]
            source = refs[job.ref].at[job.index]
            for block in range(job.blocks):
                lower = job.lower + block * job.rows
                buffer[:, block * WIDTH : (block + 1) * WIDTH] = source[
                    lower : lower + job.rows, :
                ].astype(F32)
            top = me[(2 + job.side) * PARTS + job.place] * job.rows
            if job.half is not None:
                top += (me[CORE] ^ job.side) * job.half
            where = pl.ds(pl.multiple_of(top, job.rows), job.rows)
            cols = pl.ds(job.col, job.shape[1])
            copy = pltpu.make_async_copy(
                buffer, outs[job.out].at[job.layer, where, cols], sems.at[no]
            )
            copy.start()
            copies.append(copy)
        if small:
            *halves, lower = small
            for place in range(PARTS):
                tile = refs[halves[place // 8]][place % 8, lower : lower + 16, :].astype(F32)
                rows[me[2 * PARTS + place], :, :] = tile[0:8]
            store_small(rows, refs[first + 2 : first + 2 + extra])
        for copy in copies:
            copy.wait()

    return kernel


def store_small(rows, outs):
    attn_bias, norm_gain, norm_bias, up_bias, down_bias = outs

    def row(layer, no):
        no += 10 * layer
        return rows[no // 2, no % 2 : no % 2 + 1, :]

    for layer in range(LAYERS):
        for no, source in enumerate((6, 7, 3)):
            attn_bias[no, layer : layer + 1, :] = row(layer, source)
        for no, source in enumerate((8, 1)):
            norm_gain[layer, no : no + 1, :] = row(layer, source)
        for no, source in enumerate((9, 2)):
            norm_bias[layer, no : no + 1, :] = row(layer, source)
        for no in range(2):
            up_bias[layer : layer + 1, no * WIDTH : (no + 1) * WIDTH] = row(layer, 4 + no)
        down_bias[layer : layer + 1, :] = row(layer, 0)


def call_unpack(name, me, arrays, jobs, shapes, earlier=None, small=None):
    counts = {}
    for job in jobs:
        counts[job.shape] = counts.get(job.shape, 0) + 1
    anywhere = pl.BlockSpec(memory_space=pl.ANY)
    ins = [(array, held(*array.shape)) for array in arrays]
    aliases = {}
    if earlier is not None:
        for no, array in enumerate(earlier):
            aliases[1 + len(ins)] = no
            ins.append((array, anywhere))
    outs = [((LAYERS,) + shape, F32, anywhere) for shape in shapes]
    scratch = [pltpu.VMEM((count,) + shape, F32) for shape, count in counts.items()]
    if small:
        outs += [
            (shape, F32, held(*shape))
            for shape in (
                (3, LAYERS, WIDTH), (LAYERS, 2, WIDTH), (LAYERS, 2, WIDTH),
                (LAYERS, 2 * WIDTH), (LAYERS, WIDTH),
            )
        ]
        scratch.append(pltpu.VMEM((PARTS, 8, WIDTH), F32))
    return call(
        unpack(jobs, counts, small), name, me, 1, ins, outs,
        scratch + [pltpu.SemaphoreType.DMA((len(jobs),))],
        flops=3 * 10**9, input_output_aliases=aliases,
    )


def body(
    tokens, cotangent, block_kinds, qkv_weight, out_weight, attn_bias, norm_gain, norm_bias,
    up_weight, up_bias, down_weight, down_bias,
):
    count = tokens.shape[0]
    steps = count // ROWS
    half = up_weight.shape[2]
    full = 2 * half
    mask = (jnp.asarray(mask_bias()), fixed(2, BLK, BLK))
    me = tables(lax.axis_index("dp"), lax.axis_index("mp"))

    up_other = swap_core(up_weight)
    down_other = swap_core(down_weight)
    ub_other = swap_core(up_bias)

    attn_bias = attn_bias.swapaxes(0, 1)
    ab = (attn_bias, fixed(*attn_bias.shape))
    ng = (norm_gain, fixed(*norm_gain.shape))
    nb = (norm_bias, fixed(*norm_bias.shape))
    db = (down_bias, fixed(*down_bias.shape))
    ubs = [(up_bias, fixed(*up_bias.shape)), (ub_other, fixed(*up_bias.shape))]

    def attention_weights(layer):
        return [
            (qkv_weight, of_layer(layer, WIDTH, 3 * WIDTH)),
            (out_weight, of_layer(layer, WIDTH, WIDTH)),
        ]

    def hidden_weights(layer):
        return [
            (up_weight, of_layer(layer, WIDTH, half)),
            (up_other, of_layer(layer, WIDTH, half)),
            (down_weight, of_layer(layer, half, WIDTH)),
            (down_other, of_layer(layer, half, WIDTH)),
        ]

    def rows_of(width, dtype, rows=ROWS):
        return ((count, width), dtype, tiled(width, rows))

    def blocks(array, rows=ROWS):
        return (array, tiled(array.shape[1], rows))

    qkv0, probs0, mixed0, middle0 = call(
        first_kernel, "attention_forward", block_kinds, 1,
        [mask, blocks(tokens, count)] + attention_weights(0) + [ab, ng, nb],
        [
            rows_of(3 * WIDTH, BF16, count), rows_of(HEADS * BLK, BF16, count),
            rows_of(WIDTH, BF16, count), rows_of(WIDTH, F32, count),
        ],
    )
    small_out = ((8, WIDTH), F32, held(8, WIDTH))
    cut = half // PARTS + WIDTH // PARTS * (half // WIDTH)
    part = WIDTH // 2 // PARTS

    def piece_outs(rows):
        return [
            ((PARTS, rows, WIDTH), BF16, pl.BlockSpec((PARTS, rows, WIDTH), lambda i, *_: (0, 0, 0)))
        ] * 2

    hidden_scratch = [
        pltpu.VMEM((count, full), BF16),
        pltpu.VMEM((count, full), BF16),
    ] + [pltpu.VMEM((count, WIDTH), BF16)] * 4

    few = TURN_ROWS
    later = [qkv_weight, out_weight, up_weight, up_other, down_weight, down_other]
    act0, slope0, stream1, qkv1, probs1, mixed1, output, gmid1, *pieces1, small1 = call(
        turn_kernel, "hidden_turn", me, count // few,
        [(block_kinds, pl.BlockSpec(memory_space=pltpu.SMEM)), mask]
        + [blocks(middle0, few), blocks(cotangent, few)]
        + hidden_weights(0) + [(weight, pl.BlockSpec(memory_space=pl.ANY)) for weight in later]
        + ubs + [db, ab, ng, nb],
        [
            rows_of(full, BF16, few), rows_of(full, BF16, few), rows_of(WIDTH, F32, few),
            rows_of(3 * WIDTH, BF16, few), rows_of(HEADS * BLK, BF16, few), rows_of(WIDTH, BF16, few),
            rows_of(WIDTH, BF16, few), rows_of(WIDTH, F32, few),
        ]
        + piece_outs(cut + part) + [small_out],
        [pltpu.VMEM((few, WIDTH), F32)]
        + [pltpu.VMEM(weight.shape[1:], BF16) for weight in later]
        + [pltpu.SemaphoreType.DMA((len(later),))] + hidden_scratch,
    )

    def attention_back(layer, me, gmid, mixed, qkv, probs, stream, others=()):
        return call(
            attention_backward(layer), "attention_backward", me, steps,
            [blocks(gmid), blocks(mixed), blocks(qkv), blocks(probs), blocks(stream)]
            + attention_weights(layer) + [ng, nb] + [(other, fixed(8, WIDTH)) for other in others],
            [rows_of(WIDTH, F32)] + piece_outs(4 * part if others else 3 * part) + [small_out],
            [pltpu.VMEM((count, WIDTH), BF16), pltpu.VMEM((count, 3 * WIDTH), BF16)],
            grant=GRANT[layer],
        )

    def after(value, last):
        return lax.optimization_barrier((value, last))[0]

    hidden_shapes = [(WIDTH, half), (half, WIDTH)]
    shared_shapes = [(WIDTH, 3 * WIDTH), (WIDTH, WIDTH)]
    halves = (range(8), range(8, 16))

    def hidden_jobs(layer, places):
        jobs = []
        for index, place in enumerate(places):
            jobs.append(Job(0, index, 0, half // PARTS, 1, 1, layer, place))
            jobs.append(
                Job(0, index, half // PARTS, WIDTH // PARTS, half // WIDTH, 0, layer, place)
            )
        return jobs

    def shared_jobs(out, qkv, layer, places, side):
        jobs = []
        for index, place in enumerate(places):
            jobs.append(
                Job(qkv[0], index, qkv[1], part, 3, 0, layer, place, WIDTH // 2, side)
            )
            jobs.append(
                Job(out[0], index, out[1], part, 1, 1, layer, place, WIDTH // 2, side)
            )
        return jobs

    state = {}
    transfers = {}
    results = {"hidden": None, "shared": None}

    def half_of(name, no):
        return transfers[name].result if no else transfers[name].sent

    def hidden_part(layer, no):
        value = after(half_of("p%d" % layer, no), state["last"])
        results["hidden"] = call_unpack(
            "hidden_result", me, [value], hidden_jobs(layer, halves[no]),
            hidden_shapes, results["hidden"],
        )

    def shared_part(layer, no):
        out = after(half_of("p%d" % layer, no), state["last"])
        qkv = half_of("q%d" % layer, no)
        other = swap_core(jnp.concatenate([out[:, cut:], qkv[:, : 3 * part]], axis=1))
        last = layer == 0 and no == 1
        arrays = [out, qkv, other] + ([half_of("q0", 0)] if last else [])
        results["shared"] = call_unpack(
            "shared_result", me, arrays,
            shared_jobs((0, cut), (1, 0), layer, halves[no], 0)
            + shared_jobs((2, 0), (2, part), layer, halves[no], 1),
            shared_shapes, results["shared"], (3, 1, 3 * part) if last else None,
        )

    def join(*values, skip=None):
        busy = [
            transfer
            for name, transfer in transfers.items()
            if transfer.flying is not None and name != skip
        ]
        flying = [transfer.flying for transfer in busy]
        values, flying = lax.optimization_barrier((values, flying))
        for transfer, value in zip(busy, flying):
            transfer.flying = value
        state["last"] = ()
        return values

    def start(name, pieces):
        transfers[name] = Transfer(reduce_pieces(*pieces))

    start("p1", pieces1)
    state["last"] = ()
    for step in " ".join(SCHEDULE).split():
        if step in transfers:
            state["last"] = transfers[step].advance(state["last"])
        elif step == "k4":
            grad1, *pieces, attn_small1 = attention_back(
                1, me, after(gmid1, state["last"]), mixed1, qkv1, probs1, stream1
            )
            grad1, *pieces = join(grad1, *pieces)
            start("q1", pieces)
        elif step == "k5":
            gmid0, *pieces, small0 = call(
                fifth_kernel, "hidden_backward", me, steps,
                [blocks(after(grad1, state["last"])), blocks(act0), blocks(slope0), blocks(middle0), blocks(mixed0)]
                + hidden_weights(0) + [ng, nb],
                [rows_of(WIDTH, F32)] + piece_outs(cut + part) + [small_out],
                hidden_scratch,
            )
            gmid0, *pieces = join(gmid0, *pieces)
            start("p0", pieces)
        elif step == "k6":
            grad0, *pieces, attn_small0 = attention_back(
                0, me, after(gmid0, state["last"]), mixed0, qkv0, probs0, tokens, (small0, small1, attn_small1)
            )
            grad0, *pieces = join(grad0, *pieces, skip="p0")
            start("q0", pieces)
        elif step[0] == "h":
            hidden_part(int(step[1]), int(step[2]))
            state["last"] = results["hidden"]
        else:
            shared_part(int(step[1]), int(step[2]))
            state["last"] = results["shared"]
    hidden_result = results["hidden"]
    shared_out = results["shared"]
    qkv_result, out_result, *small_results = shared_out
    attn_bias_grad, norm_gain_grad, norm_bias_grad, up_bias_grad, down_bias_grad = small_results
    return (
        output,
        grad0,
        qkv_result,
        out_result,
        attn_bias_grad.swapaxes(0, 1),
        norm_gain_grad,
        norm_bias_grad,
        hidden_result[0],
        up_bias_grad,
        hidden_result[1],
        down_bias_grad,
    )


def solution(mesh):
    placed = (
        P(("dp", "mp"), None),
        P(("dp", "mp"), None),
        P(("dp", "mp")),
        P(),
        P(),
        P(),
        P(),
        P(),
        P(None, None, "mp"),
        P(None, "mp"),
        P(None, "mp", None),
        P(),
    )
    return jax.shard_map(
        body,
        mesh=mesh,
        in_specs=placed,
        out_specs=(
            P(("dp", "mp"), None),
            P(("dp", "mp"), None),
            P(),
            P(),
            P(),
            P(),
            P(),
            P(None, None, "mp"),
            P(None, "mp"),
            P(None, "mp", None),
            P(),
        ),
        check_vma=False,
    )
```
